256 devices in a mesh: fsdp: 16 (over z, x_hi), fsdpt: 16 (over x_lo, y, core).
Axes of the slice: x: 4 (x_hi: 2, x_lo: 2; x = x_hi * 2 + x_lo), y: 4, z: 8, core: 2. Of those that a mesh axis runs over, the one named last changes fastest.
Arguments:
- tokens: bfloat16 [11264, 2304], P(('fsdpt', 'fsdp')), may hold values from -24 to 24
- gate_pre: bfloat16 [11264, 18432], P('fsdpt', 'fsdp'), may hold values from -6 to 6
- up_pre: bfloat16 [11264, 18432], P('fsdpt', 'fsdp'), may hold values from -6 to 6
- cotangent: bfloat16 [11264, 18432], P('fsdpt', 'fsdp'), may hold values from -3 to 3
- gate_weight: bfloat16 [2304, 18432], P('fsdpt', 'fsdp'), may hold values from -0.125 to 0.125
- up_weight: bfloat16 [2304, 18432], P('fsdpt', 'fsdp'), may hold values from -0.125 to 0.125
Outputs:
- input_grad: bfloat16 [11264, 2304], P(('fsdpt', 'fsdp'))
- gate_grad: bfloat16 [2304, 18432], P('fsdpt', 'fsdp')
- up_grad: bfloat16 [2304, 18432], P('fsdpt', 'fsdp')
The draws below stay inside these ranges and needn't reach their ends.
All inputs are finite; a program needn't handle non-finite values.
Results may differ from the reference program's by a relative error of at most 0.023.
Values may be sent and summed in bfloat16 or wider, within the bound.
No kernel may reach another device: no remote copies, remote signals or barrier semaphores. Data moves between devices by JAX's collectives and lax.ppermute only.
A program may use at most 128 MiB of HBM per device.

```python
import math
import jax
import jax.numpy as jnp
from jax import lax

D = 2304
FF = 18432
ROWS = 704
TOKENS = 11264
N_FSDP = 16
N_FSDPT = 16


def raised(entries, own_key, source, target, parts, factor):
    def block_of(position):
        return (jnp.arange(entries.shape[position]) // (entries.shape[position] // parts)).reshape((-1,) + (1,) * (entries.ndim - 1 - position))

    first = jax.random.permutation(own_key, parts)[block_of(target)]
    far = (block_of(target) + parts // 2) % parts
    return jnp.where((block_of(source) == first) | (block_of(source) == far), factor * entries, entries)


def steps_of(rng, dims, shards, low, top_value):
    loudness, own = 1.0, jax.random.fold_in(rng, 6)
    for axis_at, blocks in shards:
        heights = jnp.exp(jax.random.uniform(jax.random.fold_in(own, axis_at), (blocks,), jnp.float32, low / len(shards), top_value / len(shards)))
        loudness = loudness * jnp.repeat(heights, dims[axis_at] // blocks).reshape([-1 if axis == axis_at else 1 for axis in range(len(dims))])
    return loudness


def scatter_about(own_key, dims, scale, most, shards=(), held_as=jnp.bfloat16):
    gain = steps_of(own_key, dims, shards, -0.22, 0.18) if shards else 1.0
    values = jax.random.normal(own_key, dims, jnp.float32) * scale * gain
    return jnp.minimum(jnp.maximum(values, -most), most).astype(held_as)


def gaussian_with(rng, extent, scale, limit, pieces, heavy, dtype=jnp.bfloat16):
    array = scale * jax.random.normal(rng, extent, jnp.float32)
    if pieces:
        array = array * steps_of(rng, extent, pieces, -0.22, 0.18)
    return jnp.clip(raised(array, jax.random.fold_in(rng, 3), *heavy), -limit, limit).astype(dtype)


def setup_inputs(seed: int = 0) -> dict:
    streams_of = jax.random.split(jax.random.key(seed), 7)
    tokens = gaussian_with(streams_of[0], (TOKENS, D), 1.0, 24.0, ((0, 256),), (0, 1, 256, 6.0))
    gate_pre = scatter_about(streams_of[1], (TOKENS, FF), 1.0, 6.0, ((0, 16), (1, 16)))
    up_pre = scatter_about(streams_of[2], (TOKENS, FF), 1.0, 6.0, ((0, 16), (1, 16)))
    cotangent = gaussian_with(streams_of[3], (TOKENS, FF), 0.5, 3.0, ((0, 16), (1, 16)), (1, 0, 16, 2.0))
    gate_weight = scatter_about(streams_of[4], (D, FF), D ** -0.5, 0.125, ((0, 16), (1, 16)))
    up_weight = scatter_about(streams_of[5], (D, FF), D ** -0.5, 0.125, ((0, 16), (1, 16)))
    return dict(tokens=tokens, gate_pre=gate_pre, up_pre=up_pre, cotangent=cotangent, gate_weight=gate_weight, up_weight=up_weight)


def deltas(gate_pre, up_pre, cotangent):
    g = gate_pre.astype(jnp.float32)
    u = up_pre.astype(jnp.float32)
    c = cotangent.astype(jnp.float32)
    kappa = math.sqrt(2.0 / math.pi)
    tangent = jnp.tanh(kappa * (g + 0.044715 * g * g * g))
    act = 0.5 * g * (1.0 + tangent)
    slope = 0.5 * (1.0 + tangent) + 0.5 * g * (1.0 - tangent * tangent) * kappa * (1.0 + 3.0 * 0.044715 * g * g)
    return ((c * u * slope).astype(jnp.bfloat16), (c * act).astype(jnp.bfloat16))

def reference(tokens, gate_pre, up_pre, cotangent, gate_weight, up_weight):
    gate_delta, up_delta = deltas(gate_pre, up_pre, cotangent)
    hidden_block = FF // N_FSDP
    parts_g = gate_delta.reshape(TOKENS, N_FSDP, hidden_block).transpose(1, 0, 2)
    parts_u = up_delta.reshape(TOKENS, N_FSDP, hidden_block).transpose(1, 0, 2)
    parts_wg = gate_weight.reshape(D, N_FSDP, hidden_block).transpose(1, 0, 2)
    parts_wu = up_weight.reshape(D, N_FSDP, hidden_block).transpose(1, 0, 2)

    def input_step(carry, item):
        rows_g, rows_u, cols_g, cols_u = item
        partial_value = jnp.dot(rows_g, cols_g.T, preferred_element_type=jnp.float32)
        partial_value = partial_value + jnp.dot(rows_u, cols_u.T, preferred_element_type=jnp.float32)
        partial_value = lax.optimization_barrier(partial_value.astype(jnp.bfloat16))
        return (carry + partial_value.astype(jnp.float32), None)
    input_sum, unused_a = lax.scan(input_step, jnp.zeros((TOKENS, D), jnp.float32), (parts_g, parts_u, parts_wg, parts_wu))
    scale = 1.0 / math.sqrt(TOKENS)
    blocks_x = tokens.reshape(N_FSDPT, ROWS, D)
    blocks_g = gate_delta.reshape(N_FSDPT, ROWS, FF)
    blocks_u = up_delta.reshape(N_FSDPT, ROWS, FF)

    def step(carry, item):
        rows_x, rows_g, rows_u = item
        term_g = (jnp.dot(rows_x.T, rows_g, preferred_element_type=jnp.float32) * scale).astype(jnp.bfloat16)
        term_u = (jnp.dot(rows_x.T, rows_u, preferred_element_type=jnp.float32) * scale).astype(jnp.bfloat16)
        term_g, term_u = lax.optimization_barrier((term_g, term_u))
        return ((carry[0] + term_g.astype(jnp.float32), carry[1] + term_u.astype(jnp.float32)), None)
    start = (jnp.zeros((D, FF), jnp.float32), jnp.zeros((D, FF), jnp.float32))
    sums, unused = lax.scan(step, start, (blocks_x, blocks_g, blocks_u))
    return (input_sum.astype(jnp.bfloat16), sums[0].astype(jnp.bfloat16), sums[1].astype(jnp.bfloat16))
```

```python
import functools
import math

import jax
import jax.numpy as jnp
from jax import lax
from jax.experimental import pallas as pl
from jax.experimental.pallas import tpu as pltpu
from jax.sharding import Mesh, PartitionSpec as P

BF = jnp.bfloat16
F32 = jnp.float32
VMEM_LIMIT = 56 * 1024 * 1024


def shift(x, axis, k):
    n = lax.axis_size(axis)
    return lax.ppermute(x, axis, [(i, (i + k) % n) for i in range(n)])


def delta_body(z_ref, g_ref, u_ref, c_ref, out_ref):
    g = g_ref[0].astype(F32)
    u = u_ref[0].astype(F32)
    c = c_ref[0].astype(F32)
    kappa = math.sqrt(2.0 / math.pi)
    g2 = g * g
    tangent = jnp.tanh(kappa * (g + 0.044715 * g2 * g))
    half = 0.5 * (1.0 + tangent)
    act = g * half
    slope = half + 0.5 * g * (1.0 - tangent * tangent) * kappa * (1.0 + 3.0 * 0.044715 * g2)
    n = g.shape[1]
    out_ref[0, :, :n] = (c * u * slope).astype(BF)
    out_ref[0, :, n:] = (c * act).astype(BF)


def make_deltas(z, g, u, c):
    nz = lax.axis_size("z")
    rows, cols = g.shape[0] // nz, g.shape[1]
    spec = pl.BlockSpec((1, rows, cols), lambda k, zr: (lax.rem(k + zr[0], nz), 0, 0))
    return pl.pallas_call(
        delta_body,
        out_shape=jax.ShapeDtypeStruct((nz, rows, 2 * cols), BF),
        grid_spec=pltpu.PrefetchScalarGridSpec(
            num_scalar_prefetch=1,
            grid=(nz,),
            in_specs=[spec] * 3,
            out_specs=pl.BlockSpec((1, rows, 2 * cols), lambda k, zr: (k, 0, 0)),
        ),
        cost_estimate=pl.CostEstimate(
            flops=25 * g.size, bytes_accessed=10 * g.size, transcendentals=g.size
        ),
        name="deltas",
    )(z, *(a.reshape(nz, rows, cols) for a in (g, u, c)))


def split_body(blocks, s_ref, x_ref, mine_ref, other_ref):
    w = x_ref.shape[1] // (2 * blocks)
    x = x_ref[...].astype(F32)
    first = s_ref[0] == 0
    for j in range(blocks):
        a = x[:, 2 * j * w : (2 * j + 1) * w]
        b = x[:, (2 * j + 1) * w : (2 * j + 2) * w]
        mine_ref[:, j * w : (j + 1) * w] = jnp.where(first, a, b).astype(BF)
        other_ref[:, j * w : (j + 1) * w] = jnp.where(first, b, a).astype(BF)


def split_columns(core, x, blocks):
    rows, cols = x.shape
    return pl.pallas_call(
        functools.partial(split_body, blocks),
        out_shape=[jax.ShapeDtypeStruct((rows, cols // 2), BF)] * 2,
        in_specs=[
            pl.BlockSpec(memory_space=pltpu.SMEM),
            pl.BlockSpec(memory_space=pltpu.VMEM),
        ],
        out_specs=[pl.BlockSpec(memory_space=pltpu.VMEM)] * 2,
        name="split_columns",
    )(core, x)


def join_body(blocks, s_ref, a_ref, b_ref, out_ref):
    w = a_ref.shape[1] // blocks
    first = s_ref[0] == 0
    a = a_ref[...].astype(F32)
    b = b_ref[...].astype(F32)
    even = jnp.where(first, a, b)
    odd = jnp.where(first, b, a)
    for j in range(blocks):
        out_ref[:, 2 * j * w : (2 * j + 1) * w] = even[:, j * w : (j + 1) * w].astype(BF)
        out_ref[:, (2 * j + 1) * w : (2 * j + 2) * w] = odd[:, j * w : (j + 1) * w].astype(BF)


def join_columns(core, mine, other, blocks):
    rows, cols = mine.shape
    return pl.pallas_call(
        functools.partial(join_body, blocks),
        out_shape=jax.ShapeDtypeStruct((rows, 2 * cols), BF),
        in_specs=[
            pl.BlockSpec(memory_space=pltpu.SMEM),
            pl.BlockSpec(memory_space=pltpu.VMEM),
            pl.BlockSpec(memory_space=pltpu.VMEM),
        ],
        out_specs=pl.BlockSpec(memory_space=pltpu.VMEM),
        name="join_columns",
    )(core, mine, other)


def weight_body(scale, xm_ref, xo_ref, dm_ref, do_ref, out_ref):
    dims = (((0,), (0,)), ((), ()))
    acc = lax.dot_general(xm_ref[...], dm_ref[...], dims, preferred_element_type=F32)
    acc += lax.dot_general(xo_ref[...], do_ref[...], dims, preferred_element_type=F32)
    out_ref[...] = (acc * scale).astype(BF)


def weight_product(xm, xo, dm, do, scale, tile=256):
    rows, d = xm.shape
    cols = dm.shape[1]
    whole = pl.BlockSpec((rows, d), lambda i: (0, 0))
    part = pl.BlockSpec((rows, tile), lambda i: (0, i))
    return pl.pallas_call(
        functools.partial(weight_body, scale),
        out_shape=jax.ShapeDtypeStruct((d, cols), BF),
        grid=(cols // tile,),
        in_specs=[whole, whole, part, part],
        out_specs=pl.BlockSpec((d, tile), lambda i: (0, i)),
        compiler_params=pltpu.CompilerParams(vmem_limit_bytes=VMEM_LIMIT),
        cost_estimate=pl.CostEstimate(
            flops=4 * rows * d * cols,
            bytes_accessed=4 * rows * (d + cols) + 2 * d * cols,
            transcendentals=0,
        ),
        name="weight_product",
    )(xm, xo, dm, do)


def input_product(delta, w):
    return lax.dot_general(
        delta, w, (((1,), (1,)), ((), ())), preferred_element_type=F32
    ).astype(BF)


def gather_z(block):
    right, left = [block], [block]
    for _ in range(3):
        right.append(shift(right[-1], "z", 1))
        left.append(shift(left[-1], "z", -1))
    far = [shift(right[-1][0], "z", 1), shift(left[-1][1], "z", -1)]
    order = [block, left[1], left[2], left[3], far, right[3], right[2], right[1]]
    return [jnp.concatenate([b[i] for b in order], 0) for i in range(2)]


def add(*xs):
    total = xs[0].astype(F32)
    for x in xs[1:]:
        total = total + x.astype(F32)
    return total.astype(BF)


def scatter_z(mine, other):
    n = mine.shape[0] // 8

    def part(x, k):
        return x[k * n : (k + 1) * n]

    right = shift(part(mine, 4), "z", 1)
    left = shift(part(other, 4), "z", -1)
    right = jnp.stack([add(part(mine, 3), right), part(other, 3)])
    left = jnp.stack([part(mine, 5), add(part(other, 5), left)])
    right = shift(right, "z", 1)
    left = shift(left, "z", -1)
    for k in (2, 1):
        right = jnp.stack([add(part(mine, k), right[0]), add(part(other, k), right[1])])
        left = jnp.stack([add(part(mine, 8 - k), left[0]), add(part(other, 8 - k), left[1])])
        right = shift(right, "z", 1)
        left = shift(left, "z", -1)
    return [
        add(part(mine, 0), right[0], left[0]),
        add(part(other, 0), right[1], left[1]),
    ]


def per_device(tokens, gate_pre, up_pre, cotangent, gate_weight, up_weight):
    z = lax.axis_index("z")
    x_hi = lax.axis_index("x_hi")
    core = lax.axis_index("core").astype(jnp.int32).reshape(1)
    owners = lax.axis_size("x_lo") * lax.axis_size("y")
    total_tokens = gate_pre.shape[0] * owners * lax.axis_size("core")
    scale = 1.0 / math.sqrt(total_tokens)
    rows = tokens.shape[0]

    weights = lax.all_gather(
        jnp.concatenate([gate_weight, up_weight], 1), ("x_lo", "y"), axis=0, tiled=True
    )

    keep, give = split_columns(core, tokens, owners)
    pair = jnp.stack([keep, shift(give, "core", 1)])
    far = shift(pair, "x_hi", 1)
    block = jnp.where(
        x_hi == 0, jnp.concatenate([pair, far], 1), jnp.concatenate([far, pair], 1)
    )
    deltas_mine = make_deltas(z.astype(jnp.int32).reshape(1), gate_pre, up_pre, cotangent)
    deltas_mine = deltas_mine.reshape(gate_pre.shape[0], -1)
    deltas_other = shift(deltas_mine, "core", 1)
    x_mine, x_other = gather_z(block)

    product = weight_product(x_mine, x_other, deltas_mine, deltas_other, scale)
    grads = lax.psum_scatter(product, ("x_lo", "y"), scatter_dimension=0, tiled=True)

    sums = scatter_z(
        input_product(deltas_mine, weights), input_product(deltas_other, weights)
    )
    sums = jnp.stack(sums)
    low, high = sums[:, :rows], sums[:, rows:]
    sent = shift(jnp.where(x_hi == 0, high, low), "x_hi", 1)
    sums = add(jnp.where(x_hi == 0, low, high), sent)
    input_grad = join_columns(core, sums[0], shift(sums[1], "core", 1), owners)
    hidden = gate_weight.shape[1]
    return input_grad, grads[:, :hidden], grads[:, hidden:]


def solution(mesh):
    fine = Mesh(mesh.devices.reshape(8, 2, 2, 4, 2), ("z", "x_hi", "x_lo", "y", "core"))
    fsdp, fsdpt = ("z", "x_hi"), ("x_lo", "y", "core")
    both = P(fsdpt, fsdp)
    return jax.shard_map(
        per_device,
        mesh=fine,
        in_specs=(P(fsdpt + fsdp, None), both, both, both, both, both),
        out_specs=(P(fsdpt + fsdp, None), both, both),
        check_vma=False,
    )
```

```python
import functools
import math

import jax
import jax.numpy as jnp
from jax import lax
from jax.experimental import pallas as pl
from jax.experimental.pallas import tpu as pltpu
from jax.sharding import Mesh, PartitionSpec as P

BF = jnp.bfloat16
F32 = jnp.float32
VMEM_LIMIT = 56 * 1024 * 1024
IN_VMEM = pl.BlockSpec(memory_space=pltpu.VMEM)
IN_SMEM = pl.BlockSpec(memory_space=pltpu.SMEM)


def shift(x, axis, k):
    n = lax.axis_size(axis)
    return lax.ppermute(x, axis, [(i, (i + k) % n) for i in range(n)])


def add(*xs):
    total = xs[0].astype(F32)
    for x in xs[1:]:
        total = total + x.astype(F32)
    return total.astype(BF)


def delta_body(g_ref, u_ref, c_ref, out_ref):
    g = g_ref[...].astype(F32)
    u = u_ref[...].astype(F32)
    c = c_ref[...].astype(F32)
    kappa = math.sqrt(2.0 / math.pi)
    g2 = g * g
    tangent = jnp.tanh(kappa * (g + 0.044715 * g2 * g))
    half = 0.5 * (1.0 + tangent)
    act = g * half
    slope = half + 0.5 * g * (1.0 - tangent * tangent) * kappa * (1.0 + 3.0 * 0.044715 * g2)
    n = g.shape[1]
    out_ref[:, :n] = (c * u * slope).astype(BF)
    out_ref[:, n:] = (c * act).astype(BF)


def make_deltas(g, u, c, tile=64):
    rows, cols = g.shape
    spec = pl.BlockSpec((tile, cols), lambda i: (i, 0))
    return pl.pallas_call(
        delta_body,
        out_shape=jax.ShapeDtypeStruct((rows, 2 * cols), BF),
        grid=(rows // tile,),
        in_specs=[spec] * 3,
        out_specs=pl.BlockSpec((tile, 2 * cols), lambda i: (i, 0)),
        cost_estimate=pl.CostEstimate(
            flops=25 * g.size, bytes_accessed=10 * g.size, transcendentals=g.size
        ),
        name="deltas",
    )(g, u, c)


TOKEN_ORDER = ((1, 2), (0, 2), (1, 1), (1, 3), (0, 1), (0, 3), (1, 0), (0, 0))


def roll_blocks(blocks, y, sign):
    one = [jnp.where(y % 2 == 1, blocks[(i + sign) % 4], blocks[i]) for i in range(4)]
    return [jnp.where(y >= 2, one[(i + 2) % 4], one[i]) for i in range(4)]


def prologue_body(s_ref, x_ref, g_ref, u_ref, mine_ref, other_ref, w_ref):
    hidden = g_ref.shape[1]
    w_ref[:, :hidden] = g_ref[...]
    w_ref[:, hidden:] = u_ref[...]
    x_lo, y, core = s_ref[0], s_ref[1], s_ref[2]
    n = x_ref.shape[1] // 16
    x = x_ref[...].astype(F32)

    def ordered(parity):
        raw = [
            jnp.where(
                core == 0,
                x[:, (2 * j + parity) * n : (2 * j + parity + 1) * n],
                x[:, (2 * j + 1 - parity) * n : (2 * j + 2 - parity) * n],
            )
            for j in range(8)
        ]
        near = [jnp.where(x_lo == 0, raw[i], raw[i + 4]) for i in range(4)]
        far = [jnp.where(x_lo == 0, raw[i + 4], raw[i]) for i in range(4)]
        return roll_blocks(near, y, 1), roll_blocks(far, y, 1)

    for parity, ref in ((0, mine_ref), (1, other_ref)):
        by_a = ordered(parity)
        for j, (a, dy) in enumerate(TOKEN_ORDER):
            ref[:, j * n : (j + 1) * n] = by_a[a][dy].astype(BF)


def prologue(place, tokens, gate, up):
    rows, cols = tokens.shape
    half = jax.ShapeDtypeStruct((rows, cols // 2), BF)
    return pl.pallas_call(
        prologue_body,
        out_shape=[
            half,
            half,
            jax.ShapeDtypeStruct((gate.shape[0], 2 * gate.shape[1]), BF),
        ],
        in_specs=[IN_SMEM] + [IN_VMEM] * 3,
        out_specs=[IN_VMEM] * 3,
        name="prologue",
    )(place, tokens, gate, up)


def join_body(s_ref, mine_ref, other_ref, out_ref):
    x_lo, y, core = s_ref[0], s_ref[1], s_ref[2]
    n = mine_ref.shape[1] // 8

    def plain(ref):
        x = ref[...].astype(F32)
        near = roll_blocks([x[:, i * n : (i + 1) * n] for i in range(4)], y, -1)
        far = roll_blocks([x[:, (i + 4) * n : (i + 5) * n] for i in range(4)], y, -1)
        low = [jnp.where(x_lo == 0, near[i], far[i]) for i in range(4)]
        high = [jnp.where(x_lo == 0, far[i], near[i]) for i in range(4)]
        return low + high

    mine, other = plain(mine_ref), plain(other_ref)
    for j in range(8):
        out_ref[:, 2 * j * n : (2 * j + 1) * n] = jnp.where(core == 0, mine[j], other[j]).astype(BF)
        out_ref[:, (2 * j + 1) * n : (2 * j + 2) * n] = jnp.where(
            core == 0, other[j], mine[j]
        ).astype(BF)


def join_columns(place, mine, other):
    rows, cols = mine.shape
    return pl.pallas_call(
        join_body,
        out_shape=jax.ShapeDtypeStruct((rows, 2 * cols), BF),
        in_specs=[IN_SMEM, IN_VMEM, IN_VMEM],
        out_specs=IN_VMEM,
        name="join_columns",
    )(place, mine, other)


def first_body(scale, lead, xm_ref, xo_ref, dm_ref, do_ref, out_ref, xt_ref):
    rows = xm_ref.shape[0]

    @pl.when(pl.program_id(0) == 0)
    def _():
        xt_ref[:, :rows] = xm_ref[...].T
        xt_ref[:, rows:] = xo_ref[...].T

    acc = jnp.dot(xt_ref[:lead, :rows], dm_ref[...], preferred_element_type=F32)
    acc += jnp.dot(xt_ref[:lead, rows:], do_ref[...], preferred_element_type=F32)
    out_ref[...] = (acc * scale).astype(BF)


def first_product(xm, xo, dm, do, scale, lead, tile=256):
    rows, d = xm.shape
    cols = dm.shape[1]
    whole = pl.BlockSpec((rows, d), lambda i: (0, 0))
    part = pl.BlockSpec((rows, tile), lambda i: (0, i))
    return pl.pallas_call(
        functools.partial(first_body, scale, lead),
        out_shape=[
            jax.ShapeDtypeStruct((lead, cols), BF),
            jax.ShapeDtypeStruct((d, 2 * rows), BF),
        ],
        grid=(cols // tile,),
        in_specs=[whole, whole, part, part],
        out_specs=[
            pl.BlockSpec((lead, tile), lambda i: (0, i)),
            pl.BlockSpec((d, 2 * rows), lambda i: (0, 0)),
        ],
        compiler_params=pltpu.CompilerParams(vmem_limit_bytes=VMEM_LIMIT),
        cost_estimate=pl.CostEstimate(
            flops=4 * rows * lead * cols + 4 * rows * d,
            bytes_accessed=4 * rows * (2 * d + cols) + 2 * lead * cols,
            transcendentals=0,
        ),
        name="first_product",
    )(xm, xo, dm, do)


def rest_body(scale, lead, xt_ref, dm_ref, do_ref, out_ref):
    rows = dm_ref.shape[0]
    acc = jnp.dot(xt_ref[lead:, :rows], dm_ref[...], preferred_element_type=F32)
    acc += jnp.dot(xt_ref[lead:, rows:], do_ref[...], preferred_element_type=F32)
    out_ref[...] = (acc * scale).astype(BF)


def rest_product(xt, dm, do, scale, lead, tile=256):
    d = xt.shape[0]
    rows, cols = dm.shape
    part = pl.BlockSpec((rows, tile), lambda i: (0, i))
    return pl.pallas_call(
        functools.partial(rest_body, scale, lead),
        out_shape=jax.ShapeDtypeStruct((d - lead, cols), BF),
        grid=(cols // tile,),
        in_specs=[pl.BlockSpec(xt.shape, lambda i: (0, 0)), part, part],
        out_specs=pl.BlockSpec((d - lead, tile), lambda i: (0, i)),
        compiler_params=pltpu.CompilerParams(vmem_limit_bytes=VMEM_LIMIT),
        cost_estimate=pl.CostEstimate(
            flops=4 * rows * (d - lead) * cols,
            bytes_accessed=4 * rows * (d + cols) + 2 * (d - lead) * cols,
            transcendentals=0,
        ),
        name="rest_product",
    )(xt, dm, do)


def input_product(delta, w):
    return lax.dot_general(
        delta, w, (((1,), (1,)), ((), ())), preferred_element_type=F32
    ).astype(BF)


def gather_weights(w):
    far = shift(w, "x_lo", 1)
    below, above = shift(w, "y", 1), shift(w, "y", -1)
    far_below, far_above = shift(far, "y", 1), shift(far, "y", -1)
    across, far_across = shift(below, "y", 1), shift(far_above, "y", -1)
    return jnp.concatenate(
        [w, above, across, below, far, far_above, far_across, far_below], 0
    )


def scatter_grads(first, rest, n):
    rest = [rest[i * n : (i + 1) * n] for i in range(6)]
    far_up, far_down, up, down, far_own, own = rest
    far_right = shift(first[:n], "y", 1)
    left = shift(first[n:], "y", -1)
    far_left = shift(far_down, "y", -1)
    far_right = shift(add(far_up, far_right), "y", 1)
    right = shift(up, "y", 1)
    left = shift(add(down, left), "y", -1)
    far_own = shift(add(far_own, far_left, far_right), "x_lo", 1)
    return add(own, right, left, far_own)


def per_device(tokens, gate_pre, up_pre, cotangent, gate_weight, up_weight):
    x_hi = lax.axis_index("x_hi")
    place = jnp.stack([lax.axis_index(a).astype(jnp.int32) for a in ("x_lo", "y", "core")])
    total_tokens = gate_pre.shape[0] * 16
    scale = 1.0 / math.sqrt(total_tokens)
    rows = tokens.shape[0]
    owned = gate_weight.shape[0]

    keep, give, w = prologue(place, tokens, gate_weight, up_weight)
    pair = jnp.stack([keep, shift(give, "core", 1)])
    far = shift(pair, "x_hi", 1)
    block = jnp.where(
        x_hi == 0, jnp.concatenate([pair, far], 1), jnp.concatenate([far, pair], 1)
    )
    x_mine = lax.all_gather(block[0], "z", axis=0, tiled=True)
    x_other = lax.all_gather(block[1], "z", axis=0, tiled=True)

    weights = gather_weights(w)
    deltas_mine = make_deltas(gate_pre, up_pre, cotangent)
    deltas_other = shift(deltas_mine, "core", 1)

    part_mine = input_product(deltas_mine, weights)
    part_other = input_product(deltas_other, weights)
    sums = [
        lax.psum_scatter(p, "z", scatter_dimension=0, tiled=True)
        for p in (part_mine, part_other)
    ]

    first, x_t = first_product(
        x_mine, x_other, deltas_mine, deltas_other, scale, 2 * owned
    )
    rest = rest_product(x_t, deltas_mine, deltas_other, scale, 2 * owned)
    grads = scatter_grads(first, rest, owned)

    sums = jnp.stack(sums)
    low, high = sums[:, :rows], sums[:, rows:]
    sent = shift(jnp.where(x_hi == 0, high, low), "x_hi", 1)
    sums = add(jnp.where(x_hi == 0, low, high), sent)
    input_grad = join_columns(place, sums[0], shift(sums[1], "core", 1))
    hidden = gate_weight.shape[1]
    return input_grad, grads[:, :hidden], grads[:, hidden:]


def solution(mesh):
    fine = Mesh(mesh.devices.reshape(8, 2, 2, 4, 2), ("z", "x_hi", "x_lo", "y", "core"))
    fsdp, fsdpt = ("z", "x_hi"), ("x_lo", "y", "core")
    both = P(fsdpt, fsdp)
    return jax.shard_map(
        per_device,
        mesh=fine,
        in_specs=(P(fsdpt + fsdp, None), both, both, both, both, both),
        out_specs=(P(fsdpt + fsdp, None), both, both),
        check_vma=False,
    )
```

```python
import functools
import math

import jax
import jax.numpy as jnp
from jax import lax
from jax.experimental import pallas as pl
from jax.experimental.pallas import tpu as pltpu
from jax.sharding import Mesh, PartitionSpec as P

BF = jnp.bfloat16
F32 = jnp.float32
VMEM_LIMIT = 56 * 1024 * 1024
IN_VMEM = pl.BlockSpec(memory_space=pltpu.VMEM)
SMALL = pl.CostEstimate(flops=1000, bytes_accessed=1000, transcendentals=0)
INPUT_FLOPS = 1e3
DELTA_FLOPS = 1e11
REST_FLOPS = 1e11
IN_SMEM = pl.BlockSpec(memory_space=pltpu.SMEM)


def shift(x, axis, k):
    n = lax.axis_size(axis)
    return lax.ppermute(x, axis, [(i, (i + k) % n) for i in range(n)])


def add(*xs):
    total = xs[0].astype(F32)
    for x in xs[1:]:
        total = total + x.astype(F32)
    return total.astype(BF)


def delta_body(g_ref, u_ref, c_ref, out_ref):
    g = g_ref[...].astype(F32)
    u = u_ref[...].astype(F32)
    c = c_ref[...].astype(F32)
    kappa = math.sqrt(2.0 / math.pi)
    g2 = g * g
    tangent = jnp.tanh(kappa * (g + 0.044715 * g2 * g))
    half = 0.5 * (1.0 + tangent)
    act = g * half
    slope = half + 0.5 * g * (1.0 - tangent * tangent) * kappa * (1.0 + 3.0 * 0.044715 * g2)
    n = g.shape[1]
    out_ref[:, :n] = (c * u * slope).astype(BF)
    out_ref[:, n:] = (c * act).astype(BF)


def make_deltas(g, u, c, tile=176):
    rows, cols = g.shape
    spec = pl.BlockSpec((tile, cols), lambda i: (i, 0))
    return pl.pallas_call(
        delta_body,
        out_shape=jax.ShapeDtypeStruct((rows, 2 * cols), BF),
        grid=(rows // tile,),
        in_specs=[spec] * 3,
        out_specs=pl.BlockSpec((tile, 2 * cols), lambda i: (i, 0)),
        compiler_params=pltpu.CompilerParams(vmem_limit_bytes=VMEM_LIMIT),
        cost_estimate=pl.CostEstimate(flops=int(DELTA_FLOPS), bytes_accessed=1000, transcendentals=0),
        name="deltas",
    )(g, u, c)


TOKEN_ORDER = ((1, 2), (0, 2), (1, 1), (1, 3), (0, 1), (0, 3), (1, 0), (0, 0))


def roll_blocks(blocks, y, sign):
    one = [jnp.where(y % 2 == 1, blocks[(i + sign) % 4], blocks[i]) for i in range(4)]
    return [jnp.where(y >= 2, one[(i + 2) % 4], one[i]) for i in range(4)]


def pack_body(g_ref, u_ref, w_ref):
    hidden = g_ref.shape[1]
    w_ref[:, :hidden] = g_ref[...]
    w_ref[:, hidden:] = u_ref[...]


def pack_weights(gate, up):
    return pl.pallas_call(
        pack_body,
        out_shape=jax.ShapeDtypeStruct((gate.shape[0], 2 * gate.shape[1]), BF),
        in_specs=[IN_VMEM] * 2,
        out_specs=IN_VMEM,
        cost_estimate=SMALL,
        name="pack_weights",
    )(gate, up)


def split_body(s_ref, near_ref, far_ref, mine_ref, other_ref, scratch):
    x_lo, y, core, x_hi = s_ref[0], s_ref[1], s_ref[2], s_ref[3]
    rows, cols = near_ref.shape
    n = cols // 16
    near, far = near_ref[...].astype(F32), far_ref[...].astype(F32)
    for h, x in enumerate(
        (jnp.where(x_hi == 0, near, far), jnp.where(x_hi == 0, far, near))
    ):
        for parity in range(2):
            raw = [
                jnp.where(
                    core == 0,
                    x[:, (2 * j + parity) * n : (2 * j + parity + 1) * n],
                    x[:, (2 * j + 1 - parity) * n : (2 * j + 2 - parity) * n],
                )
                for j in range(8)
            ]
            close = [jnp.where(x_lo == 0, raw[i], raw[i + 4]) for i in range(4)]
            away = [jnp.where(x_lo == 0, raw[i + 4], raw[i]) for i in range(4)]
            by_a = roll_blocks(close, y, 1), roll_blocks(away, y, 1)
            for j, (a, dy) in enumerate(TOKEN_ORDER):
                scratch[parity, h * rows : (h + 1) * rows, j * n : (j + 1) * n] = by_a[a][dy]
    mine_ref[...] = scratch[0].astype(BF)
    other_ref[...] = scratch[1].astype(BF)


def split_tokens(place, near, far):
    rows, cols = near.shape
    half = jax.ShapeDtypeStruct((2 * rows, cols // 2), BF)
    return pl.pallas_call(
        split_body,
        out_shape=[half, half],
        in_specs=[IN_SMEM] + [IN_VMEM] * 2,
        out_specs=[IN_VMEM] * 2,
        scratch_shapes=[pltpu.VMEM((2, 2 * rows, cols // 2), F32)],
        cost_estimate=SMALL,
        name="split_tokens",
    )(place, near, far)


def join_body(s_ref, mine_ref, other_ref, out_ref):
    x_lo, y, core = s_ref[0], s_ref[1], s_ref[2]
    n = mine_ref.shape[1] // 8

    def plain(ref):
        x = ref[...].astype(F32)
        near = roll_blocks([x[:, i * n : (i + 1) * n] for i in range(4)], y, -1)
        far = roll_blocks([x[:, (i + 4) * n : (i + 5) * n] for i in range(4)], y, -1)
        low = [jnp.where(x_lo == 0, near[i], far[i]) for i in range(4)]
        high = [jnp.where(x_lo == 0, far[i], near[i]) for i in range(4)]
        return low + high

    mine, other = plain(mine_ref), plain(other_ref)
    for j in range(8):
        out_ref[:, 2 * j * n : (2 * j + 1) * n] = jnp.where(core == 0, mine[j], other[j]).astype(BF)
        out_ref[:, (2 * j + 1) * n : (2 * j + 2) * n] = jnp.where(
            core == 0, other[j], mine[j]
        ).astype(BF)


def join_columns(place, mine, other):
    rows, cols = mine.shape
    return pl.pallas_call(
        join_body,
        out_shape=jax.ShapeDtypeStruct((rows, 2 * cols), BF),
        in_specs=[IN_SMEM, IN_VMEM, IN_VMEM],
        out_specs=IN_VMEM,
        cost_estimate=SMALL,
        name="join_columns",
    )(place, mine, other)


def weight_body(scale, start, skip, x_ref, d_ref, *out_refs):
    n = out_refs[0].shape[0]
    acc = lax.dot_general(
        x_ref[:, start : start + skip + n * len(out_refs)],
        d_ref[...],
        (((0,), (0,)), ((), ())),
        preferred_element_type=F32,
    )
    for i, out_ref in enumerate(out_refs):
        out_ref[...] = (acc[skip + i * n : skip + (i + 1) * n] * scale).astype(BF)


def weight_product(x, delta, scale, first, count, n, cost, tile=768):
    rows, d = x.shape
    cols = delta.shape[1]
    start = first // 128 * 128
    need = -(-(first + count) // 128) * 128 if first == 0 else d
    return pl.pallas_call(
        functools.partial(weight_body, scale, start, first - start),
        out_shape=[jax.ShapeDtypeStruct((n, cols), BF)] * (count // n),
        grid=(cols // tile,),
        in_specs=[
            pl.BlockSpec((rows, need), lambda i: (0, 0)),
            pl.BlockSpec((rows, tile), lambda i: (0, i)),
        ],
        out_specs=[pl.BlockSpec((n, tile), lambda i: (0, i))] * (count // n),
        compiler_params=pltpu.CompilerParams(vmem_limit_bytes=VMEM_LIMIT),
        cost_estimate=pl.CostEstimate(
            flops=int(cost), bytes_accessed=1000, transcendentals=0
        ),
        name=f"weight_product_{first}",
    )(x, delta)


def input_body(n, *refs):
    blocks, (d_ref, out_ref, w, sems) = refs[:n], refs[n:]
    size = blocks[0].shape[0]

    @pl.when(pl.program_id(0) == 0)
    def _():
        copies = [
            pltpu.make_async_copy(b, w.at[pl.ds(i * size, size)], sems.at[i])
            for i, b in enumerate(blocks)
        ]
        for c in copies:
            c.start()
        for c in copies:
            c.wait()

    out_ref[...] = lax.dot_general(
        d_ref[...], w[...], (((1,), (1,)), ((), ())), preferred_element_type=F32
    ).astype(BF)


def input_product(delta, blocks, tile=352):
    rows, cols = delta.shape
    n = len(blocks)
    d = n * blocks[0].shape[0]
    return pl.pallas_call(
        functools.partial(input_body, n),
        out_shape=jax.ShapeDtypeStruct((rows, d), BF),
        grid=(rows // tile,),
        in_specs=[pl.BlockSpec(memory_space=pl.ANY)] * n
        + [pl.BlockSpec((tile, cols), lambda i: (i, 0))],
        out_specs=pl.BlockSpec((tile, d), lambda i: (i, 0)),
        scratch_shapes=[pltpu.VMEM((d, cols), BF), pltpu.SemaphoreType.DMA((n,))],
        compiler_params=pltpu.CompilerParams(vmem_limit_bytes=40 * 1024 * 1024),
        cost_estimate=pl.CostEstimate(flops=int(INPUT_FLOPS), bytes_accessed=1000, transcendentals=0),
        name="input_product",
    )(*blocks, delta)


def gather_weights(w, after):
    far = shift(w, "x_lo", 1)
    below, above = shift(w, "y", 1), shift(w, "y", -1)
    far, below, above, after = lax.optimization_barrier((far, below, above, after))
    far_below, far_above = shift(far, "y", 1), shift(far, "y", -1)
    across, far_across = shift(below, "y", 1), shift(far_above, "y", -1)
    return [w, above, across, below, far, far_above, far_across, far_below], after


def scatter_grads(first, rest):
    far_up, far_down, up, down, far_own, own = rest
    far_right = shift(first[0], "y", 1)
    left = shift(first[1], "y", -1)
    far_left = shift(far_down, "y", -1)
    far_right = shift(add(far_up, far_right), "y", 1)
    right = shift(up, "y", 1)
    left = shift(add(down, left), "y", -1)
    far_own = shift(add(far_own, far_left, far_right), "x_lo", 1)
    return add(own, right, left, far_own)


def per_device(tokens, gate_pre, up_pre, cotangent, gate_weight, up_weight):
    x_hi = lax.axis_index("x_hi")
    place = jnp.stack(
        [lax.axis_index(a).astype(jnp.int32) for a in ("x_lo", "y", "core", "x_hi")]
    )
    scale = 1.0 / math.sqrt(gate_pre.shape[0] * 16)
    rows, hidden = tokens.shape[0], gate_weight.shape[1]
    owned = gate_weight.shape[0]

    far_tokens = shift(tokens, "x_hi", 1)
    keep, give = split_tokens(place, tokens, far_tokens)
    block = jnp.stack([keep, shift(give, "core", 1)])
    gate_pre, block = lax.optimization_barrier((gate_pre, block))
    x = lax.all_gather(block, "z", axis=0, tiled=True).reshape(-1, keep.shape[1])
    mine = make_deltas(gate_pre, up_pre, cotangent)
    blocks, mine = gather_weights(pack_weights(gate_weight, up_weight), mine)
    other = shift(mine, "core", 1)
    delta = jnp.stack([a.reshape(8, 2 * rows, -1) for a in (mine, other)], 1)
    delta = delta.reshape(-1, 2 * hidden)

    sums = lax.psum_scatter(
        input_product(delta, blocks), "z", scatter_dimension=0, tiled=True
    )

    first = weight_product(x, delta, scale, 0, 2 * owned, owned, 1e3)
    x, first = lax.optimization_barrier((x, first))
    rest = weight_product(x, delta, scale, 2 * owned, 6 * owned, owned, REST_FLOPS)
    grads = scatter_grads(first, rest)

    sums = sums.reshape(2, 2 * rows, -1)
    low, high = sums[:, :rows], sums[:, rows:]
    sent = shift(jnp.where(x_hi == 0, high, low), "x_hi", 1)
    sums = add(jnp.where(x_hi == 0, low, high), sent)
    input_grad = join_columns(place, sums[0], shift(sums[1], "core", 1))
    return input_grad, grads[:, :hidden], grads[:, hidden:]


def solution(mesh):
    fine = Mesh(mesh.devices.reshape(8, 2, 2, 4, 2), ("z", "x_hi", "x_lo", "y", "core"))
    fsdp, fsdpt = ("z", "x_hi"), ("x_lo", "y", "core")
    both = P(fsdpt, fsdp)
    return jax.shard_map(
        per_device,
        mesh=fine,
        in_specs=(P(fsdpt + fsdp, None), both, both, both, both, both),
        out_specs=(P(fsdpt + fsdp, None), both, both),
        check_vma=False,
    )
```

```python
import functools
import math

import jax
import jax.numpy as jnp
from jax import lax
from jax.experimental import pallas as pl
from jax.experimental.pallas import tpu as pltpu
from jax.sharding import Mesh, PartitionSpec as P

BF = jnp.bfloat16
F32 = jnp.float32
VMEM_LIMIT = 56 * 1024 * 1024
IN_VMEM = pl.BlockSpec(memory_space=pltpu.VMEM)
SMALL = pl.CostEstimate(flops=1000, bytes_accessed=1000, transcendentals=0)
INPUT_FLOPS = 1e3
MARK_FLOPS = 1e12
DELTA_FLOPS = 1e11
REST_FLOPS = 1e11
IN_SMEM = pl.BlockSpec(memory_space=pltpu.SMEM)


def shift(x, axis, k):
    n = lax.axis_size(axis)
    return lax.ppermute(x, axis, [(i, (i + k) % n) for i in range(n)])


def add(*xs):
    total = xs[0].astype(F32)
    for x in xs[1:]:
        total = total + x.astype(F32)
    return total.astype(BF)


def delta_body(g_ref, u_ref, c_ref, out_ref):
    g = g_ref[...].astype(F32)
    u = u_ref[...].astype(F32)
    c = c_ref[...].astype(F32)
    kappa = math.sqrt(2.0 / math.pi)
    g2 = g * g
    tangent = jnp.tanh(kappa * (g + 0.044715 * g2 * g))
    half = 0.5 * (1.0 + tangent)
    act = g * half
    slope = half + 0.5 * g * (1.0 - tangent * tangent) * kappa * (1.0 + 3.0 * 0.044715 * g2)
    n = g.shape[1]
    out_ref[:, :n] = (c * u * slope).astype(BF)
    out_ref[:, n:] = (c * act).astype(BF)


def make_deltas(g, u, c, tile=176):
    rows, cols = g.shape
    spec = pl.BlockSpec((tile, cols), lambda i: (i, 0))
    return pl.pallas_call(
        delta_body,
        out_shape=jax.ShapeDtypeStruct((rows, 2 * cols), BF),
        grid=(rows // tile,),
        in_specs=[spec] * 3,
        out_specs=pl.BlockSpec((tile, 2 * cols), lambda i: (i, 0)),
        compiler_params=pltpu.CompilerParams(vmem_limit_bytes=VMEM_LIMIT),
        cost_estimate=pl.CostEstimate(flops=int(DELTA_FLOPS), bytes_accessed=1000, transcendentals=0),
        name="deltas",
    )(g, u, c)


def mark_body(*refs):
    refs[-1][...] = jnp.zeros_like(refs[-1])


def mark(name, *after):
    return pl.pallas_call(
        mark_body,
        out_shape=jax.ShapeDtypeStruct((8, 128), F32),
        in_specs=[pl.BlockSpec(memory_space=pl.ANY)] * len(after),
        out_specs=IN_VMEM,
        cost_estimate=pl.CostEstimate(
            flops=int(MARK_FLOPS), bytes_accessed=1000, transcendentals=0
        ),
        name=name,
    )(*after)


INPUT_ORDER = ((0, 0), (0, 1), (0, 3), (1, 0), (1, 1), (1, 3), (0, 2), (1, 2))
TOKEN_ORDER = ((1, 2), (0, 2), (1, 1), (1, 3), (0, 1), (0, 3), (1, 0), (0, 0))


def roll_blocks(blocks, y, sign):
    one = [jnp.where(y % 2 == 1, blocks[(i + sign) % 4], blocks[i]) for i in range(4)]
    return [jnp.where(y >= 2, one[(i + 2) % 4], one[i]) for i in range(4)]


def prologue_body(s_ref, x_ref, g_ref, u_ref, mine_ref, other_ref, w_ref):
    hidden = g_ref.shape[1]
    w_ref[:, :hidden] = g_ref[...]
    w_ref[:, hidden:] = u_ref[...]
    x_lo, y, core = s_ref[0], s_ref[1], s_ref[2]
    n = x_ref.shape[1] // 16
    x = x_ref[...].astype(F32)
    for parity, ref in ((0, mine_ref), (1, other_ref)):
        raw = [
            jnp.where(
                core == 0,
                x[:, (2 * j + parity) * n : (2 * j + parity + 1) * n],
                x[:, (2 * j + 1 - parity) * n : (2 * j + 2 - parity) * n],
            )
            for j in range(8)
        ]
        close = [jnp.where(x_lo == 0, raw[i], raw[i + 4]) for i in range(4)]
        away = [jnp.where(x_lo == 0, raw[i + 4], raw[i]) for i in range(4)]
        by_a = roll_blocks(close, y, 1), roll_blocks(away, y, 1)
        for j, (a, dy) in enumerate(TOKEN_ORDER):
            ref[:, j * n : (j + 1) * n] = by_a[a][dy].astype(BF)


def prologue(place, tokens, gate, up):
    rows, cols = tokens.shape
    half = jax.ShapeDtypeStruct((rows, cols // 2), BF)
    return pl.pallas_call(
        prologue_body,
        out_shape=[
            half,
            half,
            jax.ShapeDtypeStruct((gate.shape[0], 2 * gate.shape[1]), BF),
        ],
        in_specs=[IN_SMEM] + [IN_VMEM] * 3,
        out_specs=[IN_VMEM] * 3,
        cost_estimate=SMALL,
        name="prologue",
    )(place, tokens, gate, up)


def join_body(s_ref, mine_ref, other_ref, out_ref):
    x_lo, y, core = s_ref[0], s_ref[1], s_ref[2]
    n = mine_ref.shape[1] // 8

    def plain(ref):
        x = ref[...].astype(F32)
        at = {owner: x[:, j * n : (j + 1) * n] for j, owner in enumerate(INPUT_ORDER)}
        near = roll_blocks([at[0, dy] for dy in range(4)], y, -1)
        far = roll_blocks([at[1, dy] for dy in range(4)], y, -1)
        low = [jnp.where(x_lo == 0, near[i], far[i]) for i in range(4)]
        high = [jnp.where(x_lo == 0, far[i], near[i]) for i in range(4)]
        return low + high

    mine, other = plain(mine_ref), plain(other_ref)
    for j in range(8):
        out_ref[:, 2 * j * n : (2 * j + 1) * n] = jnp.where(core == 0, mine[j], other[j]).astype(BF)
        out_ref[:, (2 * j + 1) * n : (2 * j + 2) * n] = jnp.where(
            core == 0, other[j], mine[j]
        ).astype(BF)


def join_columns(place, mine, other):
    rows, cols = mine.shape
    return pl.pallas_call(
        join_body,
        out_shape=jax.ShapeDtypeStruct((rows, 2 * cols), BF),
        in_specs=[IN_SMEM, IN_VMEM, IN_VMEM],
        out_specs=IN_VMEM,
        cost_estimate=SMALL,
        name="join_columns",
    )(place, mine, other)


def weight_body(scale, start, skip, extra, x_ref, d_ref, *refs):
    out_refs = refs[extra:]
    n = out_refs[0].shape[0]
    acc = lax.dot_general(
        x_ref[:, start : start + skip + n * len(out_refs)],
        d_ref[...],
        (((0,), (0,)), ((), ())),
        preferred_element_type=F32,
    )
    for i, out_ref in enumerate(out_refs):
        out_ref[...] = (acc[skip + i * n : skip + (i + 1) * n] * scale).astype(BF)


def weight_product(x, delta, scale, first, count, n, cost, after=None, tile=768):
    rows, d = x.shape
    cols = delta.shape[1]
    start = first // 128 * 128
    need = -(-(first + count) // 128) * 128 if first == 0 else d
    after = [] if after is None else [after]
    return pl.pallas_call(
        functools.partial(weight_body, scale, start, first - start, len(after)),
        out_shape=[jax.ShapeDtypeStruct((n, cols), BF)] * (count // n),
        grid=(cols // tile,),
        in_specs=[
            pl.BlockSpec((rows, need), lambda i: (0, 0)),
            pl.BlockSpec((rows, tile), lambda i: (0, i)),
        ]
        + [pl.BlockSpec(memory_space=pl.ANY)] * len(after),
        out_specs=[pl.BlockSpec((n, tile), lambda i: (0, i))] * (count // n),
        compiler_params=pltpu.CompilerParams(vmem_limit_bytes=VMEM_LIMIT),
        cost_estimate=pl.CostEstimate(
            flops=int(cost), bytes_accessed=1000, transcendentals=0
        ),
        name=f"weight_product_{first}",
    )(x, delta, *after)


def input_body(n, done, *refs):
    blocks, refs = refs[:n], refs[n:]
    (d_ref, out_ref, w, sems), extra = refs[-4:], refs[:-4]
    size = blocks[0].shape[0]

    @pl.when(pl.program_id(0) == 0)
    def _():
        copies = [
            pltpu.make_async_copy(b, w.at[pl.ds(i * size, size)], sems.at[i])
            for i, b in enumerate(blocks)
        ]
        for c in copies:
            c.start()
        for c in copies:
            c.wait()

    if done:
        out_ref[:, :done] = extra[0][...]
    out_ref[:, done:] = lax.dot_general(
        d_ref[...], w[...], (((1,), (1,)), ((), ())), preferred_element_type=F32
    ).astype(BF)


def input_product(delta, blocks, after, cost, tile=352):
    rows, cols = delta.shape
    n = len(blocks)
    done = after.shape[1] if after.shape[0] == rows else 0
    size = n * blocks[0].shape[0]
    d = done + size
    if done:
        extra = pl.BlockSpec((tile, done), lambda i: (i, 0))
    else:
        extra = pl.BlockSpec(memory_space=pl.ANY)
    return pl.pallas_call(
        functools.partial(input_body, n, done),
        out_shape=jax.ShapeDtypeStruct((rows, d), BF),
        grid=(rows // tile,),
        in_specs=[pl.BlockSpec(memory_space=pl.ANY)] * n
        + [extra, pl.BlockSpec((tile, cols), lambda i: (i, 0))],
        out_specs=pl.BlockSpec((tile, d), lambda i: (i, 0)),
        scratch_shapes=[pltpu.VMEM((size, cols), BF), pltpu.SemaphoreType.DMA((n,))],
        compiler_params=pltpu.CompilerParams(vmem_limit_bytes=40 * 1024 * 1024),
        cost_estimate=pl.CostEstimate(
            flops=int(cost), bytes_accessed=1000, transcendentals=0
        ),
        name=f"input_product_{done}",
    )(*blocks, after, delta)


def gather_weights(w, after):
    far = shift(w, "x_lo", 1)
    below, above = shift(w, "y", 1), shift(w, "y", -1)
    far, below, above, after = lax.optimization_barrier((far, below, above, after))
    far_below, far_above = shift(far, "y", 1), shift(far, "y", -1)
    across, far_across = shift(below, "y", 1), shift(far_above, "y", -1)
    return [w, above, below, far, far_above, far_below], [across, far_across], after


def scatter_grads(first, rest):
    far_up, far_down, up, down, far_own, own = rest
    far_right = shift(first[0], "y", 1)
    left = shift(first[1], "y", -1)
    far_left = shift(far_down, "y", -1)
    far_right = shift(add(far_up, far_right), "y", 1)
    right = shift(up, "y", 1)
    left = shift(add(down, left), "y", -1)
    far_own = shift(add(far_own, far_left, far_right), "x_lo", 1)
    return add(own, right, left, far_own)


def per_device(tokens, gate_pre, up_pre, cotangent, gate_weight, up_weight):
    x_hi = lax.axis_index("x_hi")
    place = jnp.stack(
        [lax.axis_index(a).astype(jnp.int32) for a in ("x_lo", "y", "core", "x_hi")]
    )
    scale = 1.0 / math.sqrt(gate_pre.shape[0] * 16)
    rows, hidden = tokens.shape[0], gate_weight.shape[1]
    owned = gate_weight.shape[0]

    keep, give, w = prologue(place, tokens, gate_weight, up_weight)
    pair = jnp.stack([keep, shift(give, "core", 1)])
    far = shift(pair, "x_hi", 1)
    block = jnp.where(
        x_hi == 0, jnp.concatenate([pair, far], 1), jnp.concatenate([far, pair], 1)
    )
    gate_pre, block = lax.optimization_barrier((gate_pre, block))
    x = lax.all_gather(block, "z", axis=0, tiled=True).reshape(-1, keep.shape[1])
    mine = make_deltas(gate_pre, up_pre, cotangent)
    early, late, mine = gather_weights(w, mine)
    other = shift(mine, "core", 1)
    delta = jnp.stack([a.reshape(8, 2 * rows, -1) for a in (mine, other)], 1)
    delta = delta.reshape(-1, 2 * hidden)

    part = input_product(delta, early, place.reshape(1, -1), INPUT_FLOPS)
    part = input_product(delta, late, part, 1e3)
    sums = lax.psum_scatter(part, "z", scatter_dimension=0, tiled=True)

    first = weight_product(x, delta, scale, 0, 2 * owned, owned, 1e3)
    rest = weight_product(
        x, delta, scale, 2 * owned, 6 * owned, owned, REST_FLOPS, mark("sent", *first)
    )
    grads = scatter_grads(first, rest)

    sums = sums.reshape(2, 2 * rows, -1)
    low, high = sums[:, :rows], sums[:, rows:]
    sent = shift(jnp.where(x_hi == 0, high, low), "x_hi", 1)
    sums = add(jnp.where(x_hi == 0, low, high), sent)
    input_grad = join_columns(place, sums[0], shift(sums[1], "core", 1))
    return input_grad, grads[:, :hidden], grads[:, hidden:]


def solution(mesh):
    fine = Mesh(mesh.devices.reshape(8, 2, 2, 4, 2), ("z", "x_hi", "x_lo", "y", "core"))
    fsdp, fsdpt = ("z", "x_hi"), ("x_lo", "y", "core")
    both = P(fsdpt, fsdp)
    return jax.shard_map(
        per_device,
        mesh=fine,
        in_specs=(P(fsdpt + fsdp, None), both, both, both, both, both),
        out_specs=(P(fsdpt + fsdp, None), both, both),
        check_vma=False,
    )
```

```python
import functools
import math

import jax
import jax.numpy as jnp
from jax import lax
from jax.experimental import pallas as pl
from jax.experimental.pallas import tpu as pltpu
from jax.sharding import Mesh, PartitionSpec as P

BF = jnp.bfloat16
F32 = jnp.float32
VMEM_LIMIT = 56 * 1024 * 1024
IN_VMEM = pl.BlockSpec(memory_space=pltpu.VMEM)
SMALL = pl.CostEstimate(flops=1000, bytes_accessed=1000, transcendentals=0)
INPUT_FLOPS = 1e3
MARK_FLOPS = 1e12
DELTA_FLOPS = 1e11
REST_FLOPS = 1e11
IN_SMEM = pl.BlockSpec(memory_space=pltpu.SMEM)


def shift(x, axis, k):
    n = lax.axis_size(axis)
    return lax.ppermute(x, axis, [(i, (i + k) % n) for i in range(n)])


def add(*xs):
    total = xs[0].astype(F32)
    for x in xs[1:]:
        total = total + x.astype(F32)
    return total.astype(BF)


def delta_body(g_ref, u_ref, c_ref, out_ref):
    g = g_ref[...].astype(F32)
    u = u_ref[...].astype(F32)
    c = c_ref[...].astype(F32)
    kappa = math.sqrt(2.0 / math.pi)
    g2 = g * g
    tangent = jnp.tanh(kappa * (g + 0.044715 * g2 * g))
    half = 0.5 * (1.0 + tangent)
    act = g * half
    slope = half + 0.5 * g * (1.0 - tangent * tangent) * kappa * (1.0 + 3.0 * 0.044715 * g2)
    n = g.shape[1]
    out_ref[:, :n] = (c * u * slope).astype(BF)
    out_ref[:, n:] = (c * act).astype(BF)


def make_deltas(g, u, c, tile=176):
    rows, cols = g.shape
    spec = pl.BlockSpec((tile, cols), lambda i: (i, 0))
    return pl.pallas_call(
        delta_body,
        out_shape=jax.ShapeDtypeStruct((rows, 2 * cols), BF),
        grid=(rows // tile,),
        in_specs=[spec] * 3,
        out_specs=pl.BlockSpec((tile, 2 * cols), lambda i: (i, 0)),
        compiler_params=pltpu.CompilerParams(vmem_limit_bytes=VMEM_LIMIT),
        cost_estimate=pl.CostEstimate(flops=int(DELTA_FLOPS), bytes_accessed=1000, transcendentals=0),
        name="deltas",
    )(g, u, c)


def mark_body(*refs):
    refs[-1][...] = jnp.zeros_like(refs[-1])


def mark(name, *after):
    return pl.pallas_call(
        mark_body,
        out_shape=jax.ShapeDtypeStruct((8, 128), F32),
        in_specs=[pl.BlockSpec(memory_space=pl.ANY)] * len(after),
        out_specs=IN_VMEM,
        cost_estimate=pl.CostEstimate(
            flops=int(MARK_FLOPS), bytes_accessed=1000, transcendentals=0
        ),
        name=name,
    )(*after)


INPUT_ORDER = ((0, 0), (0, 1), (0, 3), (0, 2), (1, 0), (1, 1), (1, 3), (1, 2))
TOKEN_ORDER = ((1, 2), (0, 2), (1, 1), (1, 3), (0, 1), (0, 3), (1, 0), (0, 0))


def roll_blocks(blocks, y, sign):
    one = [jnp.where(y % 2 == 1, blocks[(i + sign) % 4], blocks[i]) for i in range(4)]
    return [jnp.where(y >= 2, one[(i + 2) % 4], one[i]) for i in range(4)]


def prologue_body(s_ref, x_ref, g_ref, u_ref, mine_ref, other_ref, w_ref):
    hidden = g_ref.shape[1]
    w_ref[:, :hidden] = g_ref[...]
    w_ref[:, hidden:] = u_ref[...]
    x_lo, y, core = s_ref[0], s_ref[1], s_ref[2]
    n = x_ref.shape[1] // 16
    x = x_ref[...].astype(F32)
    for parity, ref in ((0, mine_ref), (1, other_ref)):
        raw = [
            jnp.where(
                core == 0,
                x[:, (2 * j + parity) * n : (2 * j + parity + 1) * n],
                x[:, (2 * j + 1 - parity) * n : (2 * j + 2 - parity) * n],
            )
            for j in range(8)
        ]
        close = [jnp.where(x_lo == 0, raw[i], raw[i + 4]) for i in range(4)]
        away = [jnp.where(x_lo == 0, raw[i + 4], raw[i]) for i in range(4)]
        by_a = roll_blocks(close, y, 1), roll_blocks(away, y, 1)
        for j, (a, dy) in enumerate(TOKEN_ORDER):
            ref[:, j * n : (j + 1) * n] = by_a[a][dy].astype(BF)


def prologue(place, tokens, gate, up):
    rows, cols = tokens.shape
    half = jax.ShapeDtypeStruct((rows, cols // 2), BF)
    return pl.pallas_call(
        prologue_body,
        out_shape=[
            half,
            half,
            jax.ShapeDtypeStruct((gate.shape[0], 2 * gate.shape[1]), BF),
        ],
        in_specs=[IN_SMEM] + [IN_VMEM] * 3,
        out_specs=[IN_VMEM] * 3,
        cost_estimate=SMALL,
        name="prologue",
    )(place, tokens, gate, up)


def join_body(s_ref, m0_ref, m1_ref, o0_ref, o1_ref, out_ref):
    x_lo, y, core = s_ref[0], s_ref[1], s_ref[2]
    n = m0_ref.shape[1] // 8

    def plain(first, second):
        x = first[...].astype(F32) + second[...].astype(F32)
        at = {owner: x[:, j * n : (j + 1) * n] for j, owner in enumerate(INPUT_ORDER)}
        near = roll_blocks([at[0, dy] for dy in range(4)], y, -1)
        far = roll_blocks([at[1, dy] for dy in range(4)], y, -1)
        low = [jnp.where(x_lo == 0, near[i], far[i]) for i in range(4)]
        high = [jnp.where(x_lo == 0, far[i], near[i]) for i in range(4)]
        return low + high

    mine, other = plain(m0_ref, m1_ref), plain(o0_ref, o1_ref)
    for j in range(8):
        out_ref[:, 2 * j * n : (2 * j + 1) * n] = jnp.where(core == 0, mine[j], other[j]).astype(BF)
        out_ref[:, (2 * j + 1) * n : (2 * j + 2) * n] = jnp.where(
            core == 0, other[j], mine[j]
        ).astype(BF)


def join_columns(place, *parts):
    rows, cols = parts[0].shape
    return pl.pallas_call(
        join_body,
        out_shape=jax.ShapeDtypeStruct((rows, 2 * cols), BF),
        in_specs=[IN_SMEM] + [IN_VMEM] * 4,
        out_specs=IN_VMEM,
        cost_estimate=SMALL,
        name="join_columns",
    )(place, *parts)


def weight_body(scale, start, skip, extra, x_ref, d_ref, *refs):
    out_refs = refs[extra:]
    n = out_refs[0].shape[0]
    acc = lax.dot_general(
        x_ref[:, start : start + skip + n * len(out_refs)],
        d_ref[...],
        (((0,), (0,)), ((), ())),
        preferred_element_type=F32,
    )
    for i, out_ref in enumerate(out_refs):
        out_ref[...] = (acc[skip + i * n : skip + (i + 1) * n] * scale).astype(BF)


def first_body(scale, x_ref, d_ref, *out_refs):
    n = out_refs[0].shape[0]
    acc = lax.dot_general(
        x_ref[:, : n * len(out_refs) // 2],
        d_ref[...],
        (((0,), (0,)), ((), ())),
        preferred_element_type=F32,
    )
    for half in range(2):

        @pl.when(pl.program_id(0) == half)
        def _():
            for i, out_ref in enumerate(out_refs[half::2]):
                out_ref[...] = (acc[i * n : (i + 1) * n] * scale).astype(BF)


def first_product(x, delta, scale, n):
    rows = x.shape[0]
    half = delta.shape[1] // 2
    return pl.pallas_call(
        functools.partial(first_body, scale),
        out_shape=[jax.ShapeDtypeStruct((n, half), BF)] * 4,
        grid=(2,),
        in_specs=[
            pl.BlockSpec((rows, -(-2 * n // 128) * 128), lambda i: (0, 0)),
            pl.BlockSpec((rows, half), lambda i: (0, i)),
        ],
        out_specs=[pl.BlockSpec((n, half), lambda i: (0, 0))] * 4,
        compiler_params=pltpu.CompilerParams(vmem_limit_bytes=VMEM_LIMIT),
        cost_estimate=SMALL,
        name="first_product",
    )(x, delta)


def merge_body(up_ref, right_ref, down_ref, left_ref, up_out, down_out):
    half = right_ref.shape[1]
    up_out[:, :half] = (up_ref[:, :half].astype(F32) + right_ref[...].astype(F32)).astype(BF)
    up_out[:, half:] = up_ref[:, half:]
    down_out[:, :half] = down_ref[:, :half]
    down_out[:, half:] = (down_ref[:, half:].astype(F32) + left_ref[...].astype(F32)).astype(BF)


def merge(up, right, down, left):
    return pl.pallas_call(
        merge_body,
        out_shape=[jax.ShapeDtypeStruct(up.shape, BF)] * 2,
        in_specs=[IN_VMEM] * 4,
        out_specs=[IN_VMEM] * 2,
        cost_estimate=SMALL,
        name="merge",
    )(up, right, down, left)


def weight_product(x, delta, scale, first, count, n, cost, after=None, tile=768):
    rows, d = x.shape
    cols = delta.shape[1]
    start = first // 128 * 128
    need = -(-(first + count) // 128) * 128 if first == 0 else d
    after = [] if after is None else [after]
    return pl.pallas_call(
        functools.partial(weight_body, scale, start, first - start, len(after)),
        out_shape=[jax.ShapeDtypeStruct((n, cols), BF)] * (count // n),
        grid=(cols // tile,),
        in_specs=[
            pl.BlockSpec((rows, need), lambda i: (0, 0)),
            pl.BlockSpec((rows, tile), lambda i: (0, i)),
        ]
        + [pl.BlockSpec(memory_space=pl.ANY)] * len(after),
        out_specs=[pl.BlockSpec((n, tile), lambda i: (0, i))] * (count // n),
        compiler_params=pltpu.CompilerParams(vmem_limit_bytes=VMEM_LIMIT),
        cost_estimate=pl.CostEstimate(
            flops=int(cost), bytes_accessed=1000, transcendentals=0
        ),
        name=f"weight_product_{first}",
    )(x, delta, *after)


def input_body(n, done, *refs):
    blocks, refs = refs[:n], refs[n:]
    (d_ref, out_ref, w, sems), extra = refs[-4:], refs[:-4]
    size, width = blocks[0].shape
    across = w.shape[1] // width

    @pl.when(pl.program_id(0) == 0)
    def _():
        copies = [
            pltpu.make_async_copy(
                b,
                w.at[pl.ds(i // across * size, size), pl.ds(i % across * width, width)],
                sems.at[i],
            )
            for i, b in enumerate(blocks)
        ]
        for c in copies:
            c.start()
        for c in copies:
            c.wait()

    if done:
        out_ref[:, :done] = extra[0][...]
    out_ref[:, done:] = lax.dot_general(
        d_ref[...], w[...], (((1,), (1,)), ((), ())), preferred_element_type=F32
    ).astype(BF)


def input_product(delta, blocks, after, cost, tile=352):
    rows, cols = delta.shape
    n = len(blocks)
    done = after.shape[1] if after.shape[0] == rows else 0
    size = n * blocks[0].size // cols
    d = done + size
    if done:
        extra = pl.BlockSpec((tile, done), lambda i: (i, 0))
    else:
        extra = pl.BlockSpec(memory_space=pl.ANY)
    return pl.pallas_call(
        functools.partial(input_body, n, done),
        out_shape=jax.ShapeDtypeStruct((rows, d), BF),
        grid=(rows // tile,),
        in_specs=[pl.BlockSpec(memory_space=pl.ANY)] * n
        + [extra, pl.BlockSpec((tile, cols), lambda i: (i, 0))],
        out_specs=pl.BlockSpec((tile, d), lambda i: (i, 0)),
        scratch_shapes=[pltpu.VMEM((size, cols), BF), pltpu.SemaphoreType.DMA((n,))],
        compiler_params=pltpu.CompilerParams(vmem_limit_bytes=40 * 1024 * 1024),
        cost_estimate=pl.CostEstimate(
            flops=int(cost), bytes_accessed=1000, transcendentals=0
        ),
        name=f"input_product_{done}",
    )(*blocks, after, delta)


def gather_weights(w, after):
    half = w.shape[1] // 2
    far, below, above = shift(w, "x_lo", 1), shift(w, "y", 1), shift(w, "y", -1)
    far, below, above, after = lax.optimization_barrier((far, below, above, after))
    far_below, far_above = shift(below, "x_lo", 1), shift(far, "y", -1)
    across = shift(below, "y", 1)
    last = [shift(far_below[:, :half], "y", 1), shift(far_above[:, half:], "y", -1)]
    return [w, above, below, across, far, far_above, far_below], last, after


def scatter_grads(first, rest):
    far_up, far_down, up, down, far_own, own = rest
    far_right, far_left = shift(first[0], "y", 1), shift(first[1], "y", -1)
    right, left = shift(first[2], "y", 1), shift(first[3], "y", -1)
    far_up, far_down = merge(far_up, far_right, far_down, far_left)
    far_right, far_left = shift(far_up, "y", 1), shift(far_down, "y", -1)
    up, down = merge(up, right, down, left)
    up, down, far_right, far_left = lax.optimization_barrier((up, down, far_right, far_left))
    far_own = shift(add(far_own, far_left, far_right), "x_lo", 1)
    right, left = shift(up, "y", 1), shift(down, "y", -1)
    return own, right, left, far_own


def per_device(tokens, gate_pre, up_pre, cotangent, gate_weight, up_weight):
    x_hi = lax.axis_index("x_hi")
    place = jnp.stack(
        [lax.axis_index(a).astype(jnp.int32) for a in ("x_lo", "y", "core", "x_hi")]
    )
    scale = 1.0 / math.sqrt(gate_pre.shape[0] * 16)
    rows, hidden = tokens.shape[0], gate_weight.shape[1]
    owned = gate_weight.shape[0]

    keep, give, w = prologue(place, tokens, gate_weight, up_weight)
    pair = jnp.stack([keep, shift(give, "core", 1)])
    far = shift(pair, "x_hi", 1)
    block = jnp.where(
        x_hi == 0, jnp.concatenate([pair, far], 1), jnp.concatenate([far, pair], 1)
    )
    gate_pre, block = lax.optimization_barrier((gate_pre, block))
    x = lax.all_gather(block, "z", axis=0, tiled=True).reshape(-1, keep.shape[1])
    mine = make_deltas(gate_pre, up_pre, cotangent)
    early, late, mine = gather_weights(w, mine)
    other = shift(mine, "core", 1)
    delta = jnp.stack([a.reshape(8, 2 * rows, -1) for a in (mine, other)], 1)
    delta = delta.reshape(-1, 2 * hidden)

    part = input_product(delta, early, place.reshape(1, -1), INPUT_FLOPS)
    part = input_product(delta, late, part, 1e3)
    sums = lax.psum_scatter(part, "z", scatter_dimension=0, tiled=True)

    first = first_product(x, delta, scale, owned)
    rest = weight_product(
        x, delta, scale, 2 * owned, 6 * owned, owned, REST_FLOPS, mark("sent", *first)
    )
    own, *terms = scatter_grads(first, rest)

    sums = sums.reshape(2, 2, rows, -1)
    here = jnp.where(x_hi == 0, sums[:, 0], sums[:, 1])
    there = jnp.where(x_hi == 0, sums[:, 1], sums[:, 0])
    input_grad = join_columns(
        place,
        here[0],
        shift(there[0], "x_hi", 1),
        shift(here[1], "core", 1),
        lax.ppermute(there[1], ("x_hi", "core"), [(i, 3 - i) for i in range(4)]),
    )
    input_grad, own = lax.optimization_barrier((input_grad, own))
    grads = add(own, *terms)
    return input_grad, grads[:, :hidden], grads[:, hidden:]


def solution(mesh):
    fine = Mesh(mesh.devices.reshape(8, 2, 2, 4, 2), ("z", "x_hi", "x_lo", "y", "core"))
    fsdp, fsdpt = ("z", "x_hi"), ("x_lo", "y", "core")
    both = P(fsdpt, fsdp)
    return jax.shard_map(
        per_device,
        mesh=fine,
        in_specs=(P(fsdpt + fsdp, None), both, both, both, both, both),
        out_specs=(P(fsdpt + fsdp, None), both, both),
        check_vma=False,
    )
```

```python
import functools
import math

import jax
import jax.numpy as jnp
from jax import lax
from jax.experimental import pallas as pl
from jax.experimental.pallas import tpu as pltpu
from jax.sharding import Mesh, PartitionSpec as P

BF = jnp.bfloat16
F32 = jnp.float32
VMEM_LIMIT = 56 * 1024 * 1024
IN_VMEM = pl.BlockSpec(memory_space=pltpu.VMEM)
SMALL = pl.CostEstimate(flops=1000, bytes_accessed=1000, transcendentals=0)
INPUT_FLOPS = 1e3
MARK_FLOPS = 1e12
DELTA_FLOPS = 1e11
REST_FLOPS = 1e11
IN_SMEM = pl.BlockSpec(memory_space=pltpu.SMEM)


def shift(x, axis, k):
    n = lax.axis_size(axis)
    return lax.ppermute(x, axis, [(i, (i + k) % n) for i in range(n)])


def add(*xs):
    total = xs[0].astype(F32)
    for x in xs[1:]:
        total = total + x.astype(F32)
    return total.astype(BF)


def delta_body(g_ref, u_ref, c_ref, out_ref):
    g = g_ref[...].astype(F32)
    u = u_ref[...].astype(F32)
    c = c_ref[...].astype(F32)
    kappa = math.sqrt(2.0 / math.pi)
    g2 = g * g
    tangent = jnp.tanh(kappa * (g + 0.044715 * g2 * g))
    half = 0.5 * (1.0 + tangent)
    act = g * half
    slope = half + 0.5 * g * (1.0 - tangent * tangent) * kappa * (1.0 + 3.0 * 0.044715 * g2)
    n = g.shape[1]
    out_ref[:, :n] = (c * u * slope).astype(BF)
    out_ref[:, n:] = (c * act).astype(BF)


def make_deltas(g, u, c, tile=176):
    rows, cols = g.shape
    spec = pl.BlockSpec((tile, cols), lambda i: (i, 0))
    return pl.pallas_call(
        delta_body,
        out_shape=jax.ShapeDtypeStruct((rows, 2 * cols), BF),
        grid=(rows // tile,),
        in_specs=[spec] * 3,
        out_specs=pl.BlockSpec((tile, 2 * cols), lambda i: (i, 0)),
        compiler_params=pltpu.CompilerParams(vmem_limit_bytes=VMEM_LIMIT),
        cost_estimate=pl.CostEstimate(flops=int(DELTA_FLOPS), bytes_accessed=1000, transcendentals=0),
        name="deltas",
    )(g, u, c)


def mark_body(*refs):
    refs[-1][...] = jnp.zeros_like(refs[-1])


def mark(name, *after):
    return pl.pallas_call(
        mark_body,
        out_shape=jax.ShapeDtypeStruct((8, 128), F32),
        in_specs=[pl.BlockSpec(memory_space=pl.ANY)] * len(after),
        out_specs=IN_VMEM,
        cost_estimate=pl.CostEstimate(
            flops=int(MARK_FLOPS), bytes_accessed=1000, transcendentals=0
        ),
        name=name,
    )(*after)


INPUT_ORDER = ((0, 0), (0, 1), (0, 3), (0, 2), (1, 0), (1, 1), (1, 3), (1, 2))
TOKEN_ORDER = ((1, 2), (1, 1), (1, 3), (0, 2), (1, 0), (0, 1), (0, 3), (0, 0))


def roll_blocks(blocks, y, sign):
    one = [jnp.where(y % 2 == 1, blocks[(i + sign) % 4], blocks[i]) for i in range(4)]
    return [jnp.where(y >= 2, one[(i + 2) % 4], one[i]) for i in range(4)]


def prologue_body(s_ref, x_ref, g_ref, u_ref, mine_ref, other_ref, w_ref):
    hidden = g_ref.shape[1]
    w_ref[:, :hidden] = g_ref[...]
    w_ref[:, hidden:] = u_ref[...]
    x_lo, y, core = s_ref[0], s_ref[1], s_ref[2]
    n = x_ref.shape[1] // 16
    x = x_ref[...].astype(F32)
    for parity, ref in ((0, mine_ref), (1, other_ref)):
        raw = [
            jnp.where(
                core == 0,
                x[:, (2 * j + parity) * n : (2 * j + parity + 1) * n],
                x[:, (2 * j + 1 - parity) * n : (2 * j + 2 - parity) * n],
            )
            for j in range(8)
        ]
        close = [jnp.where(x_lo == 0, raw[i], raw[i + 4]) for i in range(4)]
        away = [jnp.where(x_lo == 0, raw[i + 4], raw[i]) for i in range(4)]
        by_a = roll_blocks(close, y, 1), roll_blocks(away, y, 1)
        for j, (a, dy) in enumerate(TOKEN_ORDER):
            ref[:, j * n : (j + 1) * n] = by_a[a][dy].astype(BF)


def prologue(place, tokens, gate, up):
    rows, cols = tokens.shape
    half = jax.ShapeDtypeStruct((rows, cols // 2), BF)
    return pl.pallas_call(
        prologue_body,
        out_shape=[
            half,
            half,
            jax.ShapeDtypeStruct((gate.shape[0], 2 * gate.shape[1]), BF),
        ],
        in_specs=[IN_SMEM] + [IN_VMEM] * 3,
        out_specs=[IN_VMEM] * 3,
        cost_estimate=SMALL,
        name="prologue",
    )(place, tokens, gate, up)


def join_body(s_ref, m0_ref, m1_ref, o0_ref, o1_ref, out_ref):
    x_lo, y, core = s_ref[0], s_ref[1], s_ref[2]
    n = m0_ref.shape[1] // 8

    def plain(first, second):
        x = first[...].astype(F32) + second[...].astype(F32)
        at = {owner: x[:, j * n : (j + 1) * n] for j, owner in enumerate(INPUT_ORDER)}
        near = roll_blocks([at[0, dy] for dy in range(4)], y, -1)
        far = roll_blocks([at[1, dy] for dy in range(4)], y, -1)
        low = [jnp.where(x_lo == 0, near[i], far[i]) for i in range(4)]
        high = [jnp.where(x_lo == 0, far[i], near[i]) for i in range(4)]
        return low + high

    mine, other = plain(m0_ref, m1_ref), plain(o0_ref, o1_ref)
    for j in range(8):
        out_ref[:, 2 * j * n : (2 * j + 1) * n] = jnp.where(core == 0, mine[j], other[j]).astype(BF)
        out_ref[:, (2 * j + 1) * n : (2 * j + 2) * n] = jnp.where(
            core == 0, other[j], mine[j]
        ).astype(BF)


def join_columns(place, *parts):
    rows, cols = parts[0].shape
    return pl.pallas_call(
        join_body,
        out_shape=jax.ShapeDtypeStruct((rows, 2 * cols), BF),
        in_specs=[IN_SMEM] + [IN_VMEM] * 4,
        out_specs=IN_VMEM,
        cost_estimate=SMALL,
        name="join_columns",
    )(place, *parts)


def weight_body(scale, start, skip, extra, x_ref, d_ref, *refs):
    out_refs = refs[extra:]
    n = out_refs[0].shape[0]
    acc = lax.dot_general(
        x_ref[:, start : start + skip + n * len(out_refs)],
        d_ref[...],
        (((0,), (0,)), ((), ())),
        preferred_element_type=F32,
    )
    for i, out_ref in enumerate(out_refs):
        out_ref[...] = (acc[skip + i * n : skip + (i + 1) * n] * scale).astype(BF)


def halves_body(a_ref, b_ref, gate_ref, up_ref):
    half = gate_ref.shape[1]
    gate_ref[...] = (a_ref[:, :half].astype(F32) + b_ref[:, :half].astype(F32)).astype(BF)
    up_ref[...] = (a_ref[:, half:].astype(F32) + b_ref[:, half:].astype(F32)).astype(BF)


def add_halves(a, b):
    rows, cols = a.shape
    return pl.pallas_call(
        halves_body,
        out_shape=[jax.ShapeDtypeStruct((rows, cols // 2), BF)] * 2,
        in_specs=[IN_VMEM] * 2,
        out_specs=[IN_VMEM] * 2,
        cost_estimate=SMALL,
        name="add_halves",
    )(a, b)


def merge_body(up_ref, right_ref, down_ref, left_ref, up_out, down_out):
    half = right_ref.shape[1]
    up_out[:, :half] = (up_ref[:, :half].astype(F32) + right_ref[...].astype(F32)).astype(BF)
    up_out[:, half:] = up_ref[:, half:]
    down_out[:, :half] = down_ref[:, :half]
    down_out[:, half:] = (down_ref[:, half:].astype(F32) + left_ref[...].astype(F32)).astype(BF)


def merge(up, right, down, left):
    return pl.pallas_call(
        merge_body,
        out_shape=[jax.ShapeDtypeStruct(up.shape, BF)] * 2,
        in_specs=[IN_VMEM] * 4,
        out_specs=[IN_VMEM] * 2,
        cost_estimate=SMALL,
        name="merge",
    )(up, right, down, left)


def weight_product(x, delta, scale, first, count, n, cost, after=None, tile=768):
    rows, d = x.shape
    cols = delta.shape[1]
    start = first // 128 * 128
    need = -(-(first + count) // 128) * 128 if first == 0 else d
    after = [] if after is None else [after]
    return pl.pallas_call(
        functools.partial(weight_body, scale, start, first - start, len(after)),
        out_shape=[jax.ShapeDtypeStruct((n, cols), BF)] * (count // n),
        grid=(cols // tile,),
        in_specs=[
            pl.BlockSpec((rows, need), lambda i: (0, 0)),
            pl.BlockSpec((rows, tile), lambda i: (0, i)),
        ]
        + [pl.BlockSpec(memory_space=pl.ANY)] * len(after),
        out_specs=[pl.BlockSpec((n, tile), lambda i: (0, i))] * (count // n),
        compiler_params=pltpu.CompilerParams(vmem_limit_bytes=VMEM_LIMIT),
        cost_estimate=pl.CostEstimate(
            flops=int(cost), bytes_accessed=1000, transcendentals=0
        ),
        name=f"weight_product_{first}",
    )(x, delta, *after)


def input_body(n, done, *refs):
    blocks, refs = refs[:n], refs[n:]
    (d_ref, out_ref, w, sems), extra = refs[-4:], refs[:-4]
    size, width = blocks[0].shape
    across = w.shape[1] // width

    @pl.when(pl.program_id(0) == 0)
    def _():
        copies = [
            pltpu.make_async_copy(
                b,
                w.at[pl.ds(i // across * size, size), pl.ds(i % across * width, width)],
                sems.at[i],
            )
            for i, b in enumerate(blocks)
        ]
        for c in copies:
            c.start()
        for c in copies:
            c.wait()

    if done:
        out_ref[:, :done] = extra[0][...]
    out_ref[:, done:] = lax.dot_general(
        d_ref[...], w[...], (((1,), (1,)), ((), ())), preferred_element_type=F32
    ).astype(BF)


def input_product(delta, blocks, after, cost, tile=352):
    rows, cols = delta.shape
    n = len(blocks)
    done = after.shape[1] if after.shape[0] == rows else 0
    size = n * blocks[0].size // cols
    d = done + size
    if done:
        extra = pl.BlockSpec((tile, done), lambda i: (i, 0))
    else:
        extra = pl.BlockSpec(memory_space=pl.ANY)
    return pl.pallas_call(
        functools.partial(input_body, n, done),
        out_shape=jax.ShapeDtypeStruct((rows, d), BF),
        grid=(rows // tile,),
        in_specs=[pl.BlockSpec(memory_space=pl.ANY)] * n
        + [extra, pl.BlockSpec((tile, cols), lambda i: (i, 0))],
        out_specs=pl.BlockSpec((tile, d), lambda i: (i, 0)),
        scratch_shapes=[pltpu.VMEM((size, cols), BF), pltpu.SemaphoreType.DMA((n,))],
        compiler_params=pltpu.CompilerParams(vmem_limit_bytes=40 * 1024 * 1024),
        cost_estimate=pl.CostEstimate(
            flops=int(cost), bytes_accessed=1000, transcendentals=0
        ),
        name=f"input_product_{done}",
    )(*blocks, after, delta)


def gather_weights(w, after, then):
    half = w.shape[1] // 2
    far, below, above = shift(w, "x_lo", 1), shift(w, "y", 1), shift(w, "y", -1)
    far, below, above, after = lax.optimization_barrier((far, below, above, after))
    far_below, far_above = shift(below, "x_lo", 1), shift(far, "y", -1)
    across = shift(below, "y", 1)
    then = then(after)
    far_below, far_above, then = lax.optimization_barrier((far_below, far_above, then))
    last = [shift(far_below[:, :half], "y", 1), shift(far_above[:, half:], "y", -1)]
    return [w, above, below, across, far, far_above, far_below], last, then


def scatter_grads(first, rest):
    across = shift(first[0], "x_lo", 1)
    far_right, far_left = shift(first[1], "y", 1), shift(first[2], "y", -1)
    far, far_own, up, down, own = rest
    right, left = add_halves(far, across)
    right, left = shift(right, "y", 1), shift(left, "y", -1)
    far_own = shift(add(far_own, far_left, far_right), "x_lo", 1)
    up, down = merge(up, right, down, left)
    return own, shift(up, "y", 1), shift(down, "y", -1), far_own


def per_device(tokens, gate_pre, up_pre, cotangent, gate_weight, up_weight):
    x_hi = lax.axis_index("x_hi")
    place = jnp.stack(
        [lax.axis_index(a).astype(jnp.int32) for a in ("x_lo", "y", "core", "x_hi")]
    )
    scale = 1.0 / math.sqrt(gate_pre.shape[0] * 16)
    rows, hidden = tokens.shape[0], gate_weight.shape[1]
    owned = gate_weight.shape[0]

    keep, give, w = prologue(place, tokens, gate_weight, up_weight)
    pair = jnp.stack([keep, shift(give, "core", 1)])
    far = shift(pair, "x_hi", 1)
    block = jnp.where(
        x_hi == 0, jnp.concatenate([pair, far], 1), jnp.concatenate([far, pair], 1)
    )
    gate_pre, block = lax.optimization_barrier((gate_pre, block))
    x = lax.all_gather(block, "z", axis=0, tiled=True).reshape(-1, keep.shape[1])
    mine = make_deltas(gate_pre, up_pre, cotangent)

    def both_cores(mine):
        other = shift(mine, "core", 1)
        delta = jnp.stack([a.reshape(8, 2 * rows, -1) for a in (mine, other)], 1)
        return delta.reshape(-1, 2 * hidden)

    early, late, delta = gather_weights(w, mine, both_cores)

    part = input_product(delta, early, place.reshape(1, -1), INPUT_FLOPS)
    part = input_product(delta, late, part, 1e3)
    sums = lax.psum_scatter(part, "z", scatter_dimension=0, tiled=True)

    first = weight_product(x, delta, scale, 0, 3 * owned, owned, 1e3)
    rest = weight_product(
        x, delta, scale, 3 * owned, 5 * owned, owned, REST_FLOPS, mark("sent", *first)
    )
    own, *terms = scatter_grads(first, rest)

    sums = sums.reshape(2, 2, rows, -1)
    here = jnp.where(x_hi == 0, sums[:, 0], sums[:, 1])
    there = jnp.where(x_hi == 0, sums[:, 1], sums[:, 0])
    input_grad = join_columns(
        place,
        here[0],
        shift(there[0], "x_hi", 1),
        shift(here[1], "core", 1),
        lax.ppermute(there[1], ("x_hi", "core"), [(i, 3 - i) for i in range(4)]),
    )
    input_grad, own = lax.optimization_barrier((input_grad, own))
    grads = add(own, *terms)
    return input_grad, grads[:, :hidden], grads[:, hidden:]


def solution(mesh):
    fine = Mesh(mesh.devices.reshape(8, 2, 2, 4, 2), ("z", "x_hi", "x_lo", "y", "core"))
    fsdp, fsdpt = ("z", "x_hi"), ("x_lo", "y", "core")
    both = P(fsdpt, fsdp)
    return jax.shard_map(
        per_device,
        mesh=fine,
        in_specs=(P(fsdpt + fsdp, None), both, both, both, both, both),
        out_specs=(P(fsdpt + fsdp, None), both, both),
        check_vma=False,
    )
```

```python
import functools
import math

import jax
import jax.numpy as jnp
from jax import lax
from jax.experimental import pallas as pl
from jax.experimental.pallas import tpu as pltpu
from jax.sharding import Mesh, PartitionSpec as P

BF = jnp.bfloat16
F32 = jnp.float32
VMEM_LIMIT = 56 * 1024 * 1024
IN_VMEM = pl.BlockSpec(memory_space=pltpu.VMEM)
SMALL = pl.CostEstimate(flops=1000, bytes_accessed=1000, transcendentals=0)
MARK_FLOPS = 1e12
DELTA_FLOPS = 1e11
REST_FLOPS = 1e11
IN_SMEM = pl.BlockSpec(memory_space=pltpu.SMEM)


def shift(x, axis, k):
    n = lax.axis_size(axis)
    return lax.ppermute(x, axis, [(i, (i + k) % n) for i in range(n)])


def both_flipped(x):
    return lax.ppermute(x, ("x_hi", "core"), [(i, 3 - i) for i in range(4)])


def add(*xs):
    total = xs[0].astype(F32)
    for x in xs[1:]:
        total = total + x.astype(F32)
    return total.astype(BF)


def delta_body(g_ref, u_ref, c_ref, out_ref):
    g = g_ref[...].astype(F32)
    u = u_ref[...].astype(F32)
    c = c_ref[...].astype(F32)
    kappa = math.sqrt(2.0 / math.pi)
    g2 = g * g
    tangent = jnp.tanh(kappa * (g + 0.044715 * g2 * g))
    half = 0.5 * (1.0 + tangent)
    act = g * half
    slope = half + 0.5 * g * (1.0 - tangent * tangent) * kappa * (1.0 + 3.0 * 0.044715 * g2)
    n = g.shape[1]
    out_ref[:, :n] = (c * u * slope).astype(BF)
    out_ref[:, n:] = (c * act).astype(BF)


def make_deltas(g, u, c, tile=176):
    rows, cols = g.shape
    spec = pl.BlockSpec((tile, cols), lambda i: (i, 0))
    return pl.pallas_call(
        delta_body,
        out_shape=jax.ShapeDtypeStruct((rows, 2 * cols), BF),
        grid=(rows // tile,),
        in_specs=[spec] * 3,
        out_specs=pl.BlockSpec((tile, 2 * cols), lambda i: (i, 0)),
        compiler_params=pltpu.CompilerParams(vmem_limit_bytes=VMEM_LIMIT),
        cost_estimate=pl.CostEstimate(flops=int(DELTA_FLOPS), bytes_accessed=1000, transcendentals=0),
        name="deltas",
    )(g, u, c)


def mark_body(*refs):
    refs[-1][...] = jnp.zeros_like(refs[-1])


def mark(name, *after):
    return pl.pallas_call(
        mark_body,
        out_shape=jax.ShapeDtypeStruct((8, 128), F32),
        in_specs=[pl.BlockSpec(memory_space=pl.ANY)] * len(after),
        out_specs=IN_VMEM,
        cost_estimate=pl.CostEstimate(
            flops=int(MARK_FLOPS), bytes_accessed=1000, transcendentals=0
        ),
        name=name,
    )(*after)


INPUT_ORDER = ((0, 0), (0, 1), (0, 3), (1, 0), (0, 2), (1, 1), (1, 3), (1, 2))
TOKEN_ORDER = ((1, 2), (1, 1), (1, 3), (0, 2), (1, 0), (0, 1), (0, 3), (0, 0))


def roll_blocks(blocks, y, sign):
    one = [jnp.where(y % 2 == 1, blocks[(i + sign) % 4], blocks[i]) for i in range(4)]
    return [jnp.where(y >= 2, one[(i + 2) % 4], one[i]) for i in range(4)]


def prologue_body(s_ref, x_ref, g_ref, u_ref, mine_ref, other_ref, w_ref):
    hidden = g_ref.shape[1]
    w_ref[:, :hidden] = g_ref[...]
    w_ref[:, hidden:] = u_ref[...]
    x_lo, y, core = s_ref[0], s_ref[1], s_ref[2]
    n = x_ref.shape[1] // 16
    x = x_ref[...].astype(F32)
    for parity, ref in ((0, mine_ref), (1, other_ref)):
        raw = [
            jnp.where(
                core == 0,
                x[:, (2 * j + parity) * n : (2 * j + parity + 1) * n],
                x[:, (2 * j + 1 - parity) * n : (2 * j + 2 - parity) * n],
            )
            for j in range(8)
        ]
        close = [jnp.where(x_lo == 0, raw[i], raw[i + 4]) for i in range(4)]
        away = [jnp.where(x_lo == 0, raw[i + 4], raw[i]) for i in range(4)]
        by_a = roll_blocks(close, y, 1), roll_blocks(away, y, 1)
        for j, (a, dy) in enumerate(TOKEN_ORDER):
            ref[:, j * n : (j + 1) * n] = by_a[a][dy].astype(BF)


def prologue(place, tokens, gate, up):
    rows, cols = tokens.shape
    half = jax.ShapeDtypeStruct((rows, cols // 2), BF)
    return pl.pallas_call(
        prologue_body,
        out_shape=[
            half,
            half,
            jax.ShapeDtypeStruct((gate.shape[0], 2 * gate.shape[1]), BF),
        ],
        in_specs=[IN_SMEM] + [IN_VMEM] * 3,
        out_specs=[IN_VMEM] * 3,
        cost_estimate=SMALL,
        name="prologue",
    )(place, tokens, gate, up)


def cut_body(s_ref, x_ref, m0_ref, m1_ref, o0_ref, o1_ref):
    n = m0_ref.shape[0]
    x = x_ref[...].astype(F32)
    parts = [x[i * n : (i + 1) * n] for i in range(4)]
    low = s_ref[3] == 0
    m0_ref[...] = jnp.where(low, parts[0], parts[1]).astype(BF)
    m1_ref[...] = jnp.where(low, parts[1], parts[0]).astype(BF)
    o0_ref[...] = jnp.where(low, parts[2], parts[3]).astype(BF)
    o1_ref[...] = jnp.where(low, parts[3], parts[2]).astype(BF)


def cut_sums(place, sums):
    rows, cols = sums.shape
    return pl.pallas_call(
        cut_body,
        out_shape=[jax.ShapeDtypeStruct((rows // 4, cols), BF)] * 4,
        in_specs=[IN_SMEM, IN_VMEM],
        out_specs=[IN_VMEM] * 4,
        cost_estimate=SMALL,
        name="cut_sums",
    )(place, sums)


def join_body(s_ref, m0_ref, m1_ref, o0_ref, o1_ref, out_ref):
    x_lo, y, core = s_ref[0], s_ref[1], s_ref[2]
    n = m0_ref.shape[1] // 8

    def plain(first, second):
        x = first[...].astype(F32) + second[...].astype(F32)
        at = {owner: x[:, j * n : (j + 1) * n] for j, owner in enumerate(INPUT_ORDER)}
        near = roll_blocks([at[0, dy] for dy in range(4)], y, -1)
        far = roll_blocks([at[1, dy] for dy in range(4)], y, -1)
        low = [jnp.where(x_lo == 0, near[i], far[i]) for i in range(4)]
        high = [jnp.where(x_lo == 0, far[i], near[i]) for i in range(4)]
        return low + high

    mine, other = plain(m0_ref, m1_ref), plain(o0_ref, o1_ref)
    for j in range(8):
        out_ref[:, 2 * j * n : (2 * j + 1) * n] = jnp.where(core == 0, mine[j], other[j]).astype(BF)
        out_ref[:, (2 * j + 1) * n : (2 * j + 2) * n] = jnp.where(
            core == 0, other[j], mine[j]
        ).astype(BF)


def join_columns(place, *parts):
    rows, cols = parts[0].shape
    return pl.pallas_call(
        join_body,
        out_shape=jax.ShapeDtypeStruct((rows, 2 * cols), BF),
        in_specs=[IN_SMEM] + [IN_VMEM] * 4,
        out_specs=IN_VMEM,
        cost_estimate=SMALL,
        name="join_columns",
    )(place, *parts)


def weight_body(scale, start, skip, extra, x_ref, d_ref, *refs):
    out_refs = refs[extra:]
    n = out_refs[0].shape[0]
    acc = lax.dot_general(
        x_ref[:, start : start + skip + n * len(out_refs)],
        d_ref[...],
        (((0,), (0,)), ((), ())),
        preferred_element_type=F32,
    )
    for i, out_ref in enumerate(out_refs):
        out_ref[...] = (acc[skip + i * n : skip + (i + 1) * n] * scale).astype(BF)


def halves_body(a_ref, b_ref, gate_ref, up_ref):
    half = gate_ref.shape[1]
    gate_ref[...] = (a_ref[:, :half].astype(F32) + b_ref[:, :half].astype(F32)).astype(BF)
    up_ref[...] = (a_ref[:, half:].astype(F32) + b_ref[:, half:].astype(F32)).astype(BF)


def add_halves(a, b):
    rows, cols = a.shape
    return pl.pallas_call(
        halves_body,
        out_shape=[jax.ShapeDtypeStruct((rows, cols // 2), BF)] * 2,
        in_specs=[IN_VMEM] * 2,
        out_specs=[IN_VMEM] * 2,
        cost_estimate=SMALL,
        name="add_halves",
    )(a, b)


def merge_body(up_ref, right_ref, down_ref, left_ref, up_out, down_out):
    half = right_ref.shape[1]
    up_out[:, :half] = (up_ref[:, :half].astype(F32) + right_ref[...].astype(F32)).astype(BF)
    up_out[:, half:] = up_ref[:, half:]
    down_out[:, :half] = down_ref[:, :half]
    down_out[:, half:] = (down_ref[:, half:].astype(F32) + left_ref[...].astype(F32)).astype(BF)


def merge(up, right, down, left):
    return pl.pallas_call(
        merge_body,
        out_shape=[jax.ShapeDtypeStruct(up.shape, BF)] * 2,
        in_specs=[IN_VMEM] * 4,
        out_specs=[IN_VMEM] * 2,
        cost_estimate=SMALL,
        name="merge",
    )(up, right, down, left)


def weight_product(x, delta, scale, first, count, n, cost, after=None, tile=768):
    rows, d = x.shape
    cols = delta.shape[1]
    start = first // 128 * 128
    need = min(d, -(-(first + count) // 128) * 128)
    after = [] if after is None else [after]
    return pl.pallas_call(
        functools.partial(weight_body, scale, start, first - start, len(after)),
        out_shape=[jax.ShapeDtypeStruct((n, cols), BF)] * (count // n),
        grid=(cols // tile,),
        in_specs=[
            pl.BlockSpec((rows, need), lambda i: (0, 0)),
            pl.BlockSpec((rows, tile), lambda i: (0, i)),
        ]
        + [pl.BlockSpec(memory_space=pl.ANY)] * len(after),
        out_specs=[pl.BlockSpec((n, tile), lambda i: (0, i))] * (count // n),
        compiler_params=pltpu.CompilerParams(vmem_limit_bytes=VMEM_LIMIT),
        cost_estimate=pl.CostEstimate(
            flops=int(cost), bytes_accessed=1000, transcendentals=0
        ),
        name=f"weight_product_{first}",
    )(x, delta, *after)


def input_body(n, done, *refs):
    blocks, refs = refs[:n], refs[n:]
    (d_ref, out_ref, w, sems), extra = refs[-4:], refs[:-4]
    size, width = blocks[0].shape
    across = w.shape[1] // width

    @pl.when(pl.program_id(0) == 0)
    def _():
        copies = [
            pltpu.make_async_copy(
                b,
                w.at[pl.ds(i // across * size, size), pl.ds(i % across * width, width)],
                sems.at[i],
            )
            for i, b in enumerate(blocks)
        ]
        for c in copies:
            c.start()
        for c in copies:
            c.wait()

    at = 0
    for ref in extra if done else ():
        out_ref[:, at : at + ref.shape[1]] = ref[...]
        at += ref.shape[1]
    out_ref[:, done:] = lax.dot_general(
        d_ref[...], w[...], (((1,), (1,)), ((), ())), preferred_element_type=F32
    ).astype(BF)


def input_product(delta, blocks, before=(), tile=352):
    rows, cols = delta.shape
    n = len(blocks)
    done = sum(b.shape[1] for b in before)
    size = n * blocks[0].size // cols
    d = done + size
    return pl.pallas_call(
        functools.partial(input_body, n, done),
        out_shape=jax.ShapeDtypeStruct((rows, d), BF),
        grid=(rows // tile,),
        in_specs=[pl.BlockSpec(memory_space=pl.ANY)] * n
        + [pl.BlockSpec((tile, b.shape[1]), lambda i: (i, 0)) for b in before]
        + [pl.BlockSpec((tile, cols), lambda i: (i, 0))],
        out_specs=pl.BlockSpec((tile, d), lambda i: (i, 0)),
        scratch_shapes=[pltpu.VMEM((size, cols), BF), pltpu.SemaphoreType.DMA((n,))],
        compiler_params=pltpu.CompilerParams(vmem_limit_bytes=40 * 1024 * 1024),
        cost_estimate=SMALL,
        name=f"input_product_{n}",
    )(*blocks, *before, delta)


def gather_weights(w, after, then):
    half = w.shape[1] // 2
    far, below, above = shift(w, "x_lo", 1), shift(w, "y", 1), shift(w, "y", -1)
    far, below, above, after = lax.optimization_barrier((far, below, above, after))
    far_below, far_above = shift(below, "x_lo", 1), shift(far, "y", -1)
    across = shift(below, "y", 1)
    then = then(after, [w, above, below, far])
    far_below, far_above, then = lax.optimization_barrier((far_below, far_above, then))
    last = [shift(far_below[:, :half], "y", 1), shift(far_above[:, half:], "y", -1)]
    return [across, far_above, far_below], last, then


def scatter_grads(blocks):
    across, far_up, far_down, far, far_own, up, down, own = blocks
    across = shift(across, "x_lo", 1)
    far_right, far_left = shift(far_up, "y", 1), shift(far_down, "y", -1)
    right, left = add_halves(far, across)
    right, left = shift(right, "y", 1), shift(left, "y", -1)
    far_own = shift(add(far_own, far_left, far_right), "x_lo", 1)
    up, down = merge(up, right, down, left)
    return own, shift(up, "y", 1), shift(down, "y", -1), far_own


def per_device(tokens, gate_pre, up_pre, cotangent, gate_weight, up_weight):
    x_hi = lax.axis_index("x_hi")
    place = jnp.stack(
        [lax.axis_index(a).astype(jnp.int32) for a in ("x_lo", "y", "core", "x_hi")]
    )
    scale = 1.0 / math.sqrt(gate_pre.shape[0] * 16)
    rows, hidden = tokens.shape[0], gate_weight.shape[1]
    owned = gate_weight.shape[0]

    keep, give, w = prologue(place, tokens, gate_weight, up_weight)
    pair = jnp.stack([keep, shift(give, "core", 1)])
    far = shift(pair, "x_hi", 1)
    block = jnp.where(
        x_hi == 0, jnp.concatenate([pair, far], 1), jnp.concatenate([far, pair], 1)
    )
    gate_pre, block = lax.optimization_barrier((gate_pre, block))
    x = lax.all_gather(block, "z", axis=0, tiled=True).reshape(-1, keep.shape[1])
    mine = make_deltas(gate_pre, up_pre, cotangent)

    def first_part(mine, blocks):
        other = shift(mine, "core", 1)
        delta = jnp.stack([a.reshape(8, 2 * rows, -1) for a in (mine, other)], 1)
        delta = delta.reshape(-1, 2 * hidden)
        return delta, input_product(delta, blocks)

    middle, last, (delta, part) = gather_weights(w, mine, first_part)
    part = [part, input_product(delta, middle)]
    part = input_product(delta, last, part)
    sums = lax.psum_scatter(part, "z", scatter_dimension=0, tiled=True)

    first = weight_product(x, delta, scale, 0, owned, owned, 1e3)
    middle = weight_product(
        x, delta, scale, owned, 3 * owned, owned, REST_FLOPS, mark("sent", *first)
    )
    rest = weight_product(
        x, delta, scale, 4 * owned, 4 * owned, owned, REST_FLOPS, mark("sent_too", *middle)
    )
    terms = scatter_grads(first + middle + rest)

    here, there, here_other, there_other = cut_sums(place, sums)
    parts = [here, shift(there, "x_hi", 1), both_flipped(there_other)]
    parts.append(shift(here_other, "core", 1))
    grads = add(*terms)
    grads, *parts = lax.optimization_barrier((grads, *parts))
    input_grad = join_columns(place, *parts)
    return input_grad, grads[:, :hidden], grads[:, hidden:]


def solution(mesh):
    fine = Mesh(mesh.devices.reshape(8, 2, 2, 4, 2), ("z", "x_hi", "x_lo", "y", "core"))
    fsdp, fsdpt = ("z", "x_hi"), ("x_lo", "y", "core")
    both = P(fsdpt, fsdp)
    return jax.shard_map(
        per_device,
        mesh=fine,
        in_specs=(P(fsdpt + fsdp, None), both, both, both, both, both),
        out_specs=(P(fsdpt + fsdp, None), both, both),
        check_vma=False,
    )
```

```python
import functools
import math

import jax
import jax.numpy as jnp
from jax import lax
from jax.experimental import pallas as pl
from jax.experimental.pallas import tpu as pltpu
from jax.sharding import Mesh, PartitionSpec as P

BF = jnp.bfloat16
F32 = jnp.float32
VMEM_LIMIT = 56 * 1024 * 1024
IN_VMEM = pl.BlockSpec(memory_space=pltpu.VMEM)
SMALL = pl.CostEstimate(flops=1000, bytes_accessed=1000, transcendentals=0)
MARK_FLOPS = 1e12
DELTA_FLOPS = 1e11
REST_FLOPS = 1e11


def shift(x, axis, k):
    n = lax.axis_size(axis)
    return lax.ppermute(x, axis, [(i, (i + k) % n) for i in range(n)])


def both_flipped(x):
    return lax.ppermute(x, ("x_hi", "core"), [(i, 3 - i) for i in range(4)])


def add(*xs):
    total = xs[0].astype(F32)
    for x in xs[1:]:
        total = total + x.astype(F32)
    return total.astype(BF)


def delta_body(g_ref, u_ref, c_ref, out_ref):
    g = g_ref[...].astype(F32)
    u = u_ref[...].astype(F32)
    c = c_ref[...].astype(F32)
    kappa = math.sqrt(2.0 / math.pi)
    g2 = g * g
    tangent = jnp.tanh(kappa * (g + 0.044715 * g2 * g))
    half = 0.5 * (1.0 + tangent)
    act = g * half
    slope = half + 0.5 * g * (1.0 - tangent * tangent) * kappa * (1.0 + 3.0 * 0.044715 * g2)
    n = g.shape[1]
    out_ref[:, :n] = (c * u * slope).astype(BF)
    out_ref[:, n:] = (c * act).astype(BF)


def make_deltas(g, u, c, tile=176):
    rows, cols = g.shape
    spec = pl.BlockSpec((tile, cols), lambda i: (i, 0))
    return pl.pallas_call(
        delta_body,
        out_shape=jax.ShapeDtypeStruct((rows, 2 * cols), BF),
        grid=(rows // tile,),
        in_specs=[spec] * 3,
        out_specs=pl.BlockSpec((tile, 2 * cols), lambda i: (i, 0)),
        compiler_params=pltpu.CompilerParams(vmem_limit_bytes=VMEM_LIMIT),
        cost_estimate=pl.CostEstimate(flops=int(DELTA_FLOPS), bytes_accessed=1000, transcendentals=0),
        name="deltas",
    )(g, u, c)


def mark_body(*refs):
    refs[-1][...] = jnp.zeros_like(refs[-1])


def mark(name, *after):
    return pl.pallas_call(
        mark_body,
        out_shape=jax.ShapeDtypeStruct((8, 128), F32),
        in_specs=[pl.BlockSpec(memory_space=pl.ANY)] * len(after),
        out_specs=IN_VMEM,
        cost_estimate=pl.CostEstimate(
            flops=int(MARK_FLOPS), bytes_accessed=1000, transcendentals=0
        ),
        name=name,
    )(*after)


INPUT_ORDER = ((0, 0), (1, 0), (0, 1), (0, 3), (0, 2), (1, 1), (1, 3), (1, 2))
TOKEN_ORDER = ((1, 2), (1, 1), (1, 3), (0, 2), (1, 0), (0, 1), (0, 3), (0, 0))


def roll_blocks(blocks, y, sign):
    one = [jnp.where(y % 2 == 1, blocks[(i + sign) % 4], blocks[i]) for i in range(4)]
    return [jnp.where(y >= 2, one[(i + 2) % 4], one[i]) for i in range(4)]


def prologue_body(x_ref, g_ref, u_ref, mine_ref, other_ref, w_ref):
    hidden = g_ref.shape[1]
    w_ref[:, :hidden] = g_ref[...]
    w_ref[:, hidden:] = u_ref[...]
    x_lo, y, core = (lax.axis_index(a) for a in ("x_lo", "y", "core"))
    n = x_ref.shape[1] // 16
    x = x_ref[...].astype(F32)
    for parity, ref in ((0, mine_ref), (1, other_ref)):
        raw = [
            jnp.where(
                core == 0,
                x[:, (2 * j + parity) * n : (2 * j + parity + 1) * n],
                x[:, (2 * j + 1 - parity) * n : (2 * j + 2 - parity) * n],
            )
            for j in range(8)
        ]
        close = [jnp.where(x_lo == 0, raw[i], raw[i + 4]) for i in range(4)]
        away = [jnp.where(x_lo == 0, raw[i + 4], raw[i]) for i in range(4)]
        by_a = roll_blocks(close, y, 1), roll_blocks(away, y, 1)
        for j, (a, dy) in enumerate(TOKEN_ORDER):
            ref[:, j * n : (j + 1) * n] = by_a[a][dy].astype(BF)


def prologue(tokens, gate, up):
    rows, cols = tokens.shape
    half = jax.ShapeDtypeStruct((rows, cols // 2), BF)
    return pl.pallas_call(
        prologue_body,
        out_shape=[
            half,
            half,
            jax.ShapeDtypeStruct((gate.shape[0], 2 * gate.shape[1]), BF),
        ],
        in_specs=[IN_VMEM] * 3,
        out_specs=[IN_VMEM] * 3,
        cost_estimate=SMALL,
        name="prologue",
    )(tokens, gate, up)


def cut_body(x_ref, m0_ref, m1_ref, o0_ref, o1_ref):
    n = m0_ref.shape[0]
    x = x_ref[...].astype(F32)
    parts = [x[i * n : (i + 1) * n] for i in range(4)]
    low = lax.axis_index("x_hi") == 0
    m0_ref[...] = jnp.where(low, parts[0], parts[1]).astype(BF)
    m1_ref[...] = jnp.where(low, parts[1], parts[0]).astype(BF)
    o0_ref[...] = jnp.where(low, parts[2], parts[3]).astype(BF)
    o1_ref[...] = jnp.where(low, parts[3], parts[2]).astype(BF)


def cut_sums(sums):
    rows, cols = sums.shape
    return pl.pallas_call(
        cut_body,
        out_shape=[jax.ShapeDtypeStruct((rows // 4, cols), BF)] * 4,
        in_specs=[IN_VMEM],
        out_specs=[IN_VMEM] * 4,
        cost_estimate=SMALL,
        name="cut_sums",
    )(sums)


def join_body(m0_ref, m1_ref, o0_ref, o1_ref, out_ref):
    x_lo, y, core = (lax.axis_index(a) for a in ("x_lo", "y", "core"))
    n = m0_ref.shape[1] // 8

    def plain(first, second):
        x = first[...].astype(F32) + second[...].astype(F32)
        at = {owner: x[:, j * n : (j + 1) * n] for j, owner in enumerate(INPUT_ORDER)}
        near = roll_blocks([at[0, dy] for dy in range(4)], y, -1)
        far = roll_blocks([at[1, dy] for dy in range(4)], y, -1)
        low = [jnp.where(x_lo == 0, near[i], far[i]) for i in range(4)]
        high = [jnp.where(x_lo == 0, far[i], near[i]) for i in range(4)]
        return low + high

    mine, other = plain(m0_ref, m1_ref), plain(o0_ref, o1_ref)
    for j in range(8):
        out_ref[:, 2 * j * n : (2 * j + 1) * n] = jnp.where(core == 0, mine[j], other[j]).astype(BF)
        out_ref[:, (2 * j + 1) * n : (2 * j + 2) * n] = jnp.where(
            core == 0, other[j], mine[j]
        ).astype(BF)


def join_columns(*parts):
    rows, cols = parts[0].shape
    return pl.pallas_call(
        join_body,
        out_shape=jax.ShapeDtypeStruct((rows, 2 * cols), BF),
        in_specs=[IN_VMEM] * 4,
        out_specs=IN_VMEM,
        cost_estimate=SMALL,
        name="join_columns",
    )(*parts)


def weight_body(scale, start, skip, extra, x_ref, d_ref, *refs):
    out_refs = refs[extra:]
    n = out_refs[0].shape[0]
    acc = lax.dot_general(
        x_ref[:, start : start + skip + n * len(out_refs)],
        d_ref[...],
        (((0,), (0,)), ((), ())),
        preferred_element_type=F32,
    )
    for i, out_ref in enumerate(out_refs):
        out_ref[...] = (acc[skip + i * n : skip + (i + 1) * n] * scale).astype(BF)


def halves_body(a_ref, b_ref, gate_ref, up_ref):
    half = gate_ref.shape[1]
    gate_ref[...] = (a_ref[:, :half].astype(F32) + b_ref[:, :half].astype(F32)).astype(BF)
    up_ref[...] = (a_ref[:, half:].astype(F32) + b_ref[:, half:].astype(F32)).astype(BF)


def add_halves(a, b):
    rows, cols = a.shape
    return pl.pallas_call(
        halves_body,
        out_shape=[jax.ShapeDtypeStruct((rows, cols // 2), BF)] * 2,
        in_specs=[IN_VMEM] * 2,
        out_specs=[IN_VMEM] * 2,
        cost_estimate=SMALL,
        name="add_halves",
    )(a, b)


def merge_body(up_ref, right_ref, down_ref, left_ref, up_out, down_out):
    half = right_ref.shape[1]
    up_out[:, :half] = (up_ref[:, :half].astype(F32) + right_ref[...].astype(F32)).astype(BF)
    up_out[:, half:] = up_ref[:, half:]
    down_out[:, :half] = down_ref[:, :half]
    down_out[:, half:] = (down_ref[:, half:].astype(F32) + left_ref[...].astype(F32)).astype(BF)


def merge(up, right, down, left):
    return pl.pallas_call(
        merge_body,
        out_shape=[jax.ShapeDtypeStruct(up.shape, BF)] * 2,
        in_specs=[IN_VMEM] * 4,
        out_specs=[IN_VMEM] * 2,
        cost_estimate=SMALL,
        name="merge",
    )(up, right, down, left)


def weight_product(x, delta, scale, first, count, n, cost, after=None, tile=768):
    rows, d = x.shape
    cols = delta.shape[1]
    start = first // 128 * 128
    need = min(d, -(-(first + count) // 128) * 128)
    after = [] if after is None else [after]
    return pl.pallas_call(
        functools.partial(weight_body, scale, start, first - start, len(after)),
        out_shape=[jax.ShapeDtypeStruct((n, cols), BF)] * (count // n),
        grid=(cols // tile,),
        in_specs=[
            pl.BlockSpec((rows, need), lambda i: (0, 0)),
            pl.BlockSpec((rows, tile), lambda i: (0, i)),
        ]
        + [pl.BlockSpec(memory_space=pl.ANY)] * len(after),
        out_specs=[pl.BlockSpec((n, tile), lambda i: (0, i))] * (count // n),
        compiler_params=pltpu.CompilerParams(vmem_limit_bytes=VMEM_LIMIT),
        cost_estimate=pl.CostEstimate(
            flops=int(cost), bytes_accessed=1000, transcendentals=0
        ),
        name=f"weight_product_{first}",
    )(x, delta, *after)


def input_body(n, done, *refs):
    blocks, refs = refs[:n], refs[n:]
    (d_ref, out_ref, w, sems), extra = refs[-4:], refs[:-4]
    size, width = blocks[0].shape
    across = w.shape[1] // width

    @pl.when(pl.program_id(0) == 0)
    def _():
        copies = [
            pltpu.make_async_copy(
                b,
                w.at[pl.ds(i // across * size, size), pl.ds(i % across * width, width)],
                sems.at[i],
            )
            for i, b in enumerate(blocks)
        ]
        for c in copies:
            c.start()
        for c in copies:
            c.wait()

    at = 0
    for ref in extra if done else ():
        out_ref[:, at : at + ref.shape[1]] = ref[...]
        at += ref.shape[1]
    out_ref[:, done:] = lax.dot_general(
        d_ref[...], w[...], (((1,), (1,)), ((), ())), preferred_element_type=F32
    ).astype(BF)


def input_product(delta, blocks, before=(), tile=352):
    rows, cols = delta.shape
    n = len(blocks)
    done = sum(b.shape[1] for b in before)
    size = n * blocks[0].size // cols
    d = done + size
    return pl.pallas_call(
        functools.partial(input_body, n, done),
        out_shape=jax.ShapeDtypeStruct((rows, d), BF),
        grid=(rows // tile,),
        in_specs=[pl.BlockSpec(memory_space=pl.ANY)] * n
        + [pl.BlockSpec((tile, b.shape[1]), lambda i: (i, 0)) for b in before]
        + [pl.BlockSpec((tile, cols), lambda i: (i, 0))],
        out_specs=pl.BlockSpec((tile, d), lambda i: (i, 0)),
        scratch_shapes=[pltpu.VMEM((size, cols), BF), pltpu.SemaphoreType.DMA((n,))],
        compiler_params=pltpu.CompilerParams(vmem_limit_bytes=40 * 1024 * 1024),
        cost_estimate=SMALL,
        name=f"input_product_{n}",
    )(*blocks, *before, delta)


def gather_weights(w, after, then):
    half = w.shape[1] // 2
    below, above, far = shift(w, "y", 1), shift(w, "y", -1), shift(w, "x_lo", 1)
    below, above, far, after = lax.optimization_barrier((below, above, far, after))
    far_below, far_above = shift(below, "x_lo", 1), shift(far, "y", -1)
    across = shift(below, "y", 1)
    then = then(after, [w, far, above, below])
    far_below, far_above, then = lax.optimization_barrier((far_below, far_above, then))
    last = [shift(far_below[:, :half], "y", 1), shift(far_above[:, half:], "y", -1)]
    return [across, far_above, far_below], last, then


def scatter_grads(blocks, others):
    across, far_up, far_down, far, far_own = blocks
    across = shift(across, "x_lo", 1)
    far_right, far_left = shift(far_up, "y", 1), shift(far_down, "y", -1)
    halves = add_halves(far, across)
    up, down, own = others(*halves)
    right, left = shift(halves[0], "y", 1), shift(halves[1], "y", -1)
    far_own = shift(add(far_own, far_left, far_right), "x_lo", 1)
    up, down = merge(up, right, down, left)
    return own, shift(up, "y", 1), shift(down, "y", -1), far_own


def per_device(tokens, gate_pre, up_pre, cotangent, gate_weight, up_weight):
    x_hi = lax.axis_index("x_hi")
    scale = 1.0 / math.sqrt(gate_pre.shape[0] * 16)
    rows, hidden = tokens.shape[0], gate_weight.shape[1]
    owned = gate_weight.shape[0]

    keep, give, w = prologue(tokens, gate_weight, up_weight)
    pair = jnp.stack([keep, shift(give, "core", 1)])
    far = shift(pair, "x_hi", 1)
    block = jnp.where(
        x_hi == 0, jnp.concatenate([pair, far], 1), jnp.concatenate([far, pair], 1)
    )
    gate_pre, block = lax.optimization_barrier((gate_pre, block))
    x = lax.all_gather(block, "z", axis=0, tiled=True).reshape(-1, keep.shape[1])
    mine = make_deltas(gate_pre, up_pre, cotangent)

    def first_part(mine, blocks):
        other = shift(mine, "core", 1)
        delta = jnp.stack([a.reshape(8, 2 * rows, -1) for a in (mine, other)], 1)
        delta = delta.reshape(-1, 2 * hidden)
        return delta, input_product(delta, blocks)

    middle, last, (delta, part) = gather_weights(w, mine, first_part)
    part = [part, input_product(delta, middle)]
    part = input_product(delta, last, part)
    sums = lax.psum_scatter(part, "z", scatter_dimension=0, tiled=True)

    first = weight_product(x, delta, scale, 0, owned, owned, 1e3, tile=hidden)
    middle = weight_product(
        x, delta, scale, owned, 4 * owned, owned, REST_FLOPS, mark("sent", *first)
    )

    def last_products(*after):
        return weight_product(
            x, delta, scale, 5 * owned, 3 * owned, owned, REST_FLOPS, mark("sent_too", *after)
        )

    terms = scatter_grads(first + middle, last_products)

    here, there, here_other, there_other = cut_sums(sums)
    parts = [here, shift(there, "x_hi", 1), both_flipped(there_other)]
    parts.append(shift(here_other, "core", 1))
    grads = add(*terms)
    grads, *parts = lax.optimization_barrier((grads, *parts))
    input_grad = join_columns(*parts)
    return input_grad, grads[:, :hidden], grads[:, hidden:]


def solution(mesh):
    fine = Mesh(mesh.devices.reshape(8, 2, 2, 4, 2), ("z", "x_hi", "x_lo", "y", "core"))
    fsdp, fsdpt = ("z", "x_hi"), ("x_lo", "y", "core")
    both = P(fsdpt, fsdp)
    return jax.shard_map(
        per_device,
        mesh=fine,
        in_specs=(P(fsdpt + fsdp, None), both, both, both, both, both),
        out_specs=(P(fsdpt + fsdp, None), both, both),
        check_vma=False,
    )
```

```python
import functools
import math

import jax
import jax.numpy as jnp
from jax import lax
from jax.experimental import pallas as pl
from jax.experimental.pallas import tpu as pltpu
from jax.sharding import Mesh, PartitionSpec as P

BF = jnp.bfloat16
F32 = jnp.float32
VMEM_LIMIT = 56 * 1024 * 1024
IN_VMEM = pl.BlockSpec(memory_space=pltpu.VMEM)
SMALL = pl.CostEstimate(flops=1000, bytes_accessed=1000, transcendentals=0)
MARK_FLOPS = 1e12
DELTA_FLOPS = 1e11
REST_FLOPS = 1e11


def shift(x, axis, k):
    n = lax.axis_size(axis)
    return lax.ppermute(x, axis, [(i, (i + k) % n) for i in range(n)])


def both_flipped(x):
    return lax.ppermute(x, ("x_hi", "core"), [(i, 3 - i) for i in range(4)])


def add(*xs):
    total = xs[0].astype(F32)
    for x in xs[1:]:
        total = total + x.astype(F32)
    return total.astype(BF)


def delta_body(z_ref, g_ref, u_ref, c_ref, out_ref):
    g = g_ref[0].astype(F32)
    u = u_ref[0].astype(F32)
    c = c_ref[0].astype(F32)
    kappa = math.sqrt(2.0 / math.pi)
    g2 = g * g
    tangent = jnp.tanh(kappa * (g + 0.044715 * g2 * g))
    half = 0.5 * (1.0 + tangent)
    act = g * half
    slope = half + 0.5 * g * (1.0 - tangent * tangent) * kappa * (1.0 + 3.0 * 0.044715 * g2)
    n = g.shape[1]
    out_ref[0, :, :n] = (c * u * slope).astype(BF)
    out_ref[0, :, n:] = (c * act).astype(BF)


def make_deltas(z, g, u, c):
    nz = lax.axis_size("z")
    rows, cols = g.shape[0] // nz, g.shape[1]
    spec = pl.BlockSpec((1, rows, cols), lambda k, zr: (lax.rem(k + zr[0], nz), 0, 0))
    return pl.pallas_call(
        delta_body,
        out_shape=jax.ShapeDtypeStruct((nz, rows, 2 * cols), BF),
        grid_spec=pltpu.PrefetchScalarGridSpec(
            num_scalar_prefetch=1,
            grid=(nz,),
            in_specs=[spec] * 3,
            out_specs=pl.BlockSpec((1, rows, 2 * cols), lambda k, zr: (k, 0, 0)),
        ),
        cost_estimate=pl.CostEstimate(
            flops=int(DELTA_FLOPS), bytes_accessed=1000, transcendentals=0
        ),
        name="deltas",
    )(z, *(a.reshape(nz, rows, cols) for a in (g, u, c)))


def mark_body(*refs):
    refs[-1][...] = jnp.zeros_like(refs[-1])


def mark(name, *after):
    return pl.pallas_call(
        mark_body,
        out_shape=jax.ShapeDtypeStruct((8, 128), F32),
        in_specs=[pl.BlockSpec(memory_space=pl.ANY)] * len(after),
        out_specs=IN_VMEM,
        cost_estimate=pl.CostEstimate(
            flops=int(MARK_FLOPS), bytes_accessed=1000, transcendentals=0
        ),
        name=name,
    )(*after)


INPUT_ORDER = ((0, 0), (1, 0), (0, 1), (0, 3), (0, 2), (1, 1), (1, 3), (1, 2))
TOKEN_ORDER = ((1, 2), (1, 1), (1, 3), (0, 2), (1, 0), (0, 1), (0, 3), (0, 0))


def roll_blocks(blocks, y, sign):
    one = [jnp.where(y % 2 == 1, blocks[(i + sign) % 4], blocks[i]) for i in range(4)]
    return [jnp.where(y >= 2, one[(i + 2) % 4], one[i]) for i in range(4)]


def prologue_body(x_ref, g_ref, u_ref, mine_ref, other_ref, w_ref):
    hidden = g_ref.shape[1]
    w_ref[:, :hidden] = g_ref[...]
    w_ref[:, hidden:] = u_ref[...]
    x_lo, y, core = (lax.axis_index(a) for a in ("x_lo", "y", "core"))
    n = x_ref.shape[1] // 16
    x = x_ref[...].astype(F32)
    for parity, ref in ((0, mine_ref), (1, other_ref)):
        raw = [
            jnp.where(
                core == 0,
                x[:, (2 * j + parity) * n : (2 * j + parity + 1) * n],
                x[:, (2 * j + 1 - parity) * n : (2 * j + 2 - parity) * n],
            )
            for j in range(8)
        ]
        close = [jnp.where(x_lo == 0, raw[i], raw[i + 4]) for i in range(4)]
        away = [jnp.where(x_lo == 0, raw[i + 4], raw[i]) for i in range(4)]
        by_a = roll_blocks(close, y, 1), roll_blocks(away, y, 1)
        for j, (a, dy) in enumerate(TOKEN_ORDER):
            ref[:, j * n : (j + 1) * n] = by_a[a][dy].astype(BF)


def prologue(tokens, gate, up):
    rows, cols = tokens.shape
    half = jax.ShapeDtypeStruct((rows, cols // 2), BF)
    return pl.pallas_call(
        prologue_body,
        out_shape=[
            half,
            half,
            jax.ShapeDtypeStruct((gate.shape[0], 2 * gate.shape[1]), BF),
        ],
        in_specs=[IN_VMEM] * 3,
        out_specs=[IN_VMEM] * 3,
        cost_estimate=SMALL,
        name="prologue",
    )(tokens, gate, up)


def cut_body(x_ref, m0_ref, m1_ref, o0_ref, o1_ref):
    n = m0_ref.shape[0]
    x = x_ref[...].astype(F32)
    parts = [x[i * n : (i + 1) * n] for i in range(4)]
    low = lax.axis_index("x_hi") == 0
    m0_ref[...] = jnp.where(low, parts[0], parts[1]).astype(BF)
    m1_ref[...] = jnp.where(low, parts[1], parts[0]).astype(BF)
    o0_ref[...] = jnp.where(low, parts[2], parts[3]).astype(BF)
    o1_ref[...] = jnp.where(low, parts[3], parts[2]).astype(BF)


def cut_sums(sums):
    rows, cols = sums.shape
    return pl.pallas_call(
        cut_body,
        out_shape=[jax.ShapeDtypeStruct((rows // 4, cols), BF)] * 4,
        in_specs=[IN_VMEM],
        out_specs=[IN_VMEM] * 4,
        cost_estimate=SMALL,
        name="cut_sums",
    )(sums)


def join_body(m0_ref, m1_ref, o0_ref, o1_ref, out_ref):
    x_lo, y, core = (lax.axis_index(a) for a in ("x_lo", "y", "core"))
    n = m0_ref.shape[1] // 8

    def plain(first, second):
        x = first[...].astype(F32) + second[...].astype(F32)
        at = {owner: x[:, j * n : (j + 1) * n] for j, owner in enumerate(INPUT_ORDER)}
        near = roll_blocks([at[0, dy] for dy in range(4)], y, -1)
        far = roll_blocks([at[1, dy] for dy in range(4)], y, -1)
        low = [jnp.where(x_lo == 0, near[i], far[i]) for i in range(4)]
        high = [jnp.where(x_lo == 0, far[i], near[i]) for i in range(4)]
        return low + high

    mine, other = plain(m0_ref, m1_ref), plain(o0_ref, o1_ref)
    for j in range(8):
        out_ref[:, 2 * j * n : (2 * j + 1) * n] = jnp.where(core == 0, mine[j], other[j]).astype(BF)
        out_ref[:, (2 * j + 1) * n : (2 * j + 2) * n] = jnp.where(
            core == 0, other[j], mine[j]
        ).astype(BF)


def join_columns(*parts):
    rows, cols = parts[0].shape
    return pl.pallas_call(
        join_body,
        out_shape=jax.ShapeDtypeStruct((rows, 2 * cols), BF),
        in_specs=[IN_VMEM] * 4,
        out_specs=IN_VMEM,
        cost_estimate=SMALL,
        name="join_columns",
    )(*parts)


def weight_body(scale, start, skip, extra, x_ref, d_ref, *refs):
    out_refs = refs[extra:]
    n = out_refs[0].shape[0]
    acc = lax.dot_general(
        x_ref[:, start : start + skip + n * len(out_refs)],
        d_ref[...],
        (((0,), (0,)), ((), ())),
        preferred_element_type=F32,
    )
    for i, out_ref in enumerate(out_refs):
        out_ref[...] = (acc[skip + i * n : skip + (i + 1) * n] * scale).astype(BF)


def halves_body(a_ref, b_ref, gate_ref, up_ref):
    half = gate_ref.shape[1]
    gate_ref[...] = (a_ref[:, :half].astype(F32) + b_ref[:, :half].astype(F32)).astype(BF)
    up_ref[...] = (a_ref[:, half:].astype(F32) + b_ref[:, half:].astype(F32)).astype(BF)


def add_halves(a, b):
    rows, cols = a.shape
    return pl.pallas_call(
        halves_body,
        out_shape=[jax.ShapeDtypeStruct((rows, cols // 2), BF)] * 2,
        in_specs=[IN_VMEM] * 2,
        out_specs=[IN_VMEM] * 2,
        cost_estimate=SMALL,
        name="add_halves",
    )(a, b)


def merge_body(up_ref, right_ref, down_ref, left_ref, up_out, down_out):
    half = right_ref.shape[1]
    up_out[:, :half] = (up_ref[:, :half].astype(F32) + right_ref[...].astype(F32)).astype(BF)
    up_out[:, half:] = up_ref[:, half:]
    down_out[:, :half] = down_ref[:, :half]
    down_out[:, half:] = (down_ref[:, half:].astype(F32) + left_ref[...].astype(F32)).astype(BF)


def merge(up, right, down, left):
    return pl.pallas_call(
        merge_body,
        out_shape=[jax.ShapeDtypeStruct(up.shape, BF)] * 2,
        in_specs=[IN_VMEM] * 4,
        out_specs=[IN_VMEM] * 2,
        cost_estimate=SMALL,
        name="merge",
    )(up, right, down, left)


def weight_product(x, delta, scale, first, count, n, cost, after=None, tile=768):
    rows, d = x.shape
    cols = delta.shape[1]
    start = first // 128 * 128
    need = min(d, -(-(first + count) // 128) * 128)
    after = [] if after is None else [after]
    return pl.pallas_call(
        functools.partial(weight_body, scale, start, first - start, len(after)),
        out_shape=[jax.ShapeDtypeStruct((n, cols), BF)] * (count // n),
        grid=(cols // tile,),
        in_specs=[
            pl.BlockSpec((rows, need), lambda i: (0, 0)),
            pl.BlockSpec((rows, tile), lambda i: (0, i)),
        ]
        + [pl.BlockSpec(memory_space=pl.ANY)] * len(after),
        out_specs=[pl.BlockSpec((n, tile), lambda i: (0, i))] * (count // n),
        compiler_params=pltpu.CompilerParams(vmem_limit_bytes=VMEM_LIMIT),
        cost_estimate=pl.CostEstimate(
            flops=int(cost), bytes_accessed=1000, transcendentals=0
        ),
        name=f"weight_product_{first}",
    )(x, delta, *after)


def input_body(n, done, *refs):
    blocks, refs = refs[:n], refs[n:]
    (d_ref, out_ref, w, sems), extra = refs[-4:], refs[:-4]
    size, width = blocks[0].shape
    across = w.shape[1] // width

    @pl.when(pl.program_id(0) == 0)
    def _():
        copies = [
            pltpu.make_async_copy(
                b,
                w.at[pl.ds(i // across * size, size), pl.ds(i % across * width, width)],
                sems.at[i],
            )
            for i, b in enumerate(blocks)
        ]
        for c in copies:
            c.start()
        for c in copies:
            c.wait()

    at = 0
    for ref in extra if done else ():
        out_ref[:, at : at + ref.shape[1]] = ref[...]
        at += ref.shape[1]
    out_ref[:, done:] = lax.dot_general(
        d_ref[...], w[...], (((1,), (1,)), ((), ())), preferred_element_type=F32
    ).astype(BF)


def input_product(delta, blocks, before=(), tile=352):
    rows, cols = delta.shape
    n = len(blocks)
    done = sum(b.shape[1] for b in before)
    size = n * blocks[0].size // cols
    d = done + size
    return pl.pallas_call(
        functools.partial(input_body, n, done),
        out_shape=jax.ShapeDtypeStruct((rows, d), BF),
        grid=(rows // tile,),
        in_specs=[pl.BlockSpec(memory_space=pl.ANY)] * n
        + [pl.BlockSpec((tile, b.shape[1]), lambda i: (i, 0)) for b in before]
        + [pl.BlockSpec((tile, cols), lambda i: (i, 0))],
        out_specs=pl.BlockSpec((tile, d), lambda i: (i, 0)),
        scratch_shapes=[pltpu.VMEM((size, cols), BF), pltpu.SemaphoreType.DMA((n,))],
        compiler_params=pltpu.CompilerParams(vmem_limit_bytes=40 * 1024 * 1024),
        cost_estimate=SMALL,
        name=f"input_product_{n}",
    )(*blocks, *before, delta)


def gather_weights(w, after, then):
    half = w.shape[1] // 2
    below, above, far = shift(w, "y", 1), shift(w, "y", -1), shift(w, "x_lo", 1)
    below, above, far, after = lax.optimization_barrier((below, above, far, after))
    far_below, far_above = shift(below, "x_lo", 1), shift(far, "y", -1)
    across = shift(below, "y", 1)
    then = then(after, [w, far, above, below])
    far_below, far_above, then = lax.optimization_barrier((far_below, far_above, then))
    last = [shift(far_below[:, :half], "y", 1), shift(far_above[:, half:], "y", -1)]
    return [across, far_above, far_below], last, then


def scatter_grads(blocks):
    across, far_up, far_down, far, far_own, up, down, own = blocks
    across = shift(across, "x_lo", 1)
    far_right, far_left = shift(far_up, "y", 1), shift(far_down, "y", -1)
    across, far_right, far_left = lax.optimization_barrier((across, far_right, far_left))
    right, left = add_halves(far, across)
    right, left = shift(right, "y", 1), shift(left, "y", -1)
    far_own = shift(add(far_own, far_left, far_right), "x_lo", 1)
    up, down = merge(up, right, down, left)
    return own, shift(up, "y", 1), shift(down, "y", -1), far_own


def both_ways(right, left):
    return shift(right, "z", 1), shift(left, "z", -1)


def gather_far(right, left):
    n = right.shape[0] // 2
    return both_ways(right[:n], left[n:])


def scatter_z(x):
    size = x.shape[0] // 8
    n = size // 2
    part = [x[k * size : (k + 1) * size] for k in range(8)]
    right, left = lax.optimization_barrier(both_ways(part[4][:n], part[4][n:]))
    right = jnp.concatenate([add(part[3][:n], right), part[3][n:]])
    left = jnp.concatenate([part[5][:n], add(part[5][n:], left)])
    for k in (2, 1, 0):
        right, left = lax.optimization_barrier(both_ways(right, left))
        if k:
            right, left = add(part[k], right), add(part[8 - k], left)
    return add(part[0], right, left)


def per_device(tokens, gate_pre, up_pre, cotangent, gate_weight, up_weight):
    x_hi = lax.axis_index("x_hi")
    scale = 1.0 / math.sqrt(gate_pre.shape[0] * 16)
    rows, hidden = tokens.shape[0], gate_weight.shape[1]
    owned = gate_weight.shape[0]

    keep, give, w = prologue(tokens, gate_weight, up_weight)
    pair = jnp.stack([keep, shift(give, "core", 1)])
    far = shift(pair, "x_hi", 1)
    block = jnp.where(
        x_hi == 0, jnp.concatenate([pair, far], 1), jnp.concatenate([far, pair], 1)
    )
    gate_pre, block = lax.optimization_barrier((gate_pre, block))
    block = block.reshape(-1, keep.shape[1])
    one = both_ways(block, block)
    z = lax.axis_index("z").astype(jnp.int32).reshape(1)
    mine = make_deltas(z, gate_pre, up_pre, cotangent)
    *one, mine = lax.optimization_barrier((*one, mine))
    two = both_ways(*one)

    def first_part(mine, blocks):
        other = shift(mine, "core", 1)
        delta = jnp.stack([mine, other], 1)
        delta = delta.reshape(-1, 2 * hidden)
        return delta, input_product(delta, blocks)

    middle, last, (delta, part) = gather_weights(w, mine, first_part)
    *two, part = lax.optimization_barrier((*two, part))
    three = both_ways(*two)
    far = gather_far(*three)
    x = jnp.concatenate([block, one[1], two[1], three[1], *far, three[0], two[0], one[0]], 0)
    part = [part, input_product(delta, middle)]
    part = input_product(delta, last, part)
    sums = scatter_z(part)

    first = weight_product(x, delta, scale, 0, 3 * owned, owned, 1e3, tile=hidden)
    rest = weight_product(
        x, delta, scale, 3 * owned, 5 * owned, owned, REST_FLOPS, mark("sent", *first)
    )
    terms = scatter_grads(first + rest)

    here, there, here_other, there_other = cut_sums(sums)
    parts = [here, shift(there, "x_hi", 1), both_flipped(there_other)]
    parts.append(shift(here_other, "core", 1))
    grads = add(*terms)
    grads, *parts = lax.optimization_barrier((grads, *parts))
    input_grad = join_columns(*parts)
    return input_grad, grads[:, :hidden], grads[:, hidden:]


def solution(mesh):
    fine = Mesh(mesh.devices.reshape(8, 2, 2, 4, 2), ("z", "x_hi", "x_lo", "y", "core"))
    fsdp, fsdpt = ("z", "x_hi"), ("x_lo", "y", "core")
    both = P(fsdpt, fsdp)
    return jax.shard_map(
        per_device,
        mesh=fine,
        in_specs=(P(fsdpt + fsdp, None), both, both, both, both, both),
        out_specs=(P(fsdpt + fsdp, None), both, both),
        check_vma=False,
    )
```

```python
import functools
import math

import jax
import jax.numpy as jnp
from jax import lax
from jax.experimental import pallas as pl
from jax.experimental.pallas import tpu as pltpu
from jax.sharding import Mesh, PartitionSpec as P

BF = jnp.bfloat16
F32 = jnp.float32
VMEM_LIMIT = 56 * 1024 * 1024
IN_VMEM = pl.BlockSpec(memory_space=pltpu.VMEM)
SMALL = pl.CostEstimate(flops=1000, bytes_accessed=1000, transcendentals=0)
MARK_FLOPS = 1e12
DELTA_FLOPS = 1e11
REST_FLOPS = 1e11


def shift(x, axis, k):
    n = lax.axis_size(axis)
    return lax.ppermute(x, axis, [(i, (i + k) % n) for i in range(n)])


def both_flipped(x):
    return lax.ppermute(x, ("x_hi", "core"), [(i, 3 - i) for i in range(4)])


def add(*xs):
    total = xs[0].astype(F32)
    for x in xs[1:]:
        total = total + x.astype(F32)
    return total.astype(BF)


def delta_body(g_ref, u_ref, c_ref, out_ref):
    g = g_ref[...].astype(F32)
    u = u_ref[...].astype(F32)
    c = c_ref[...].astype(F32)
    kappa = math.sqrt(2.0 / math.pi)
    g2 = g * g
    tangent = jnp.tanh(kappa * (g + 0.044715 * g2 * g))
    half = 0.5 * (1.0 + tangent)
    act = g * half
    slope = half + 0.5 * g * (1.0 - tangent * tangent) * kappa * (1.0 + 3.0 * 0.044715 * g2)
    n = g.shape[1]
    out_ref[:, :n] = (c * u * slope).astype(BF)
    out_ref[:, n:] = (c * act).astype(BF)


def make_deltas(g, u, c, tile=176):
    rows, cols = g.shape
    spec = pl.BlockSpec((tile, cols), lambda i: (i, 0))
    return pl.pallas_call(
        delta_body,
        out_shape=jax.ShapeDtypeStruct((rows, 2 * cols), BF),
        grid=(rows // tile,),
        in_specs=[spec] * 3,
        out_specs=pl.BlockSpec((tile, 2 * cols), lambda i: (i, 0)),
        compiler_params=pltpu.CompilerParams(vmem_limit_bytes=VMEM_LIMIT),
        cost_estimate=pl.CostEstimate(flops=int(DELTA_FLOPS), bytes_accessed=1000, transcendentals=0),
        name="deltas",
    )(g, u, c)


def mark_body(*refs):
    refs[-1][...] = jnp.zeros_like(refs[-1])


def mark(name, *after):
    return pl.pallas_call(
        mark_body,
        out_shape=jax.ShapeDtypeStruct((8, 128), F32),
        in_specs=[pl.BlockSpec(memory_space=pl.ANY)] * len(after),
        out_specs=IN_VMEM,
        cost_estimate=pl.CostEstimate(
            flops=int(MARK_FLOPS), bytes_accessed=1000, transcendentals=0
        ),
        name=name,
    )(*after)


INPUT_ORDER = ((0, 0), (1, 0), (0, 1), (0, 3), (0, 2), (1, 1), (1, 3), (1, 2))
TOKEN_ORDER = ((1, 2), (1, 1), (1, 3), (0, 2), (1, 0), (0, 1), (0, 3), (0, 0))


def roll_blocks(blocks, y, sign):
    one = [jnp.where(y % 2 == 1, blocks[(i + sign) % 4], blocks[i]) for i in range(4)]
    return [jnp.where(y >= 2, one[(i + 2) % 4], one[i]) for i in range(4)]


def prologue_body(x_ref, g_ref, u_ref, mine_ref, other_ref, w_ref):
    hidden = g_ref.shape[1]
    w_ref[:, :hidden] = g_ref[...]
    w_ref[:, hidden:] = u_ref[...]
    x_lo, y, core = (lax.axis_index(a) for a in ("x_lo", "y", "core"))
    n = x_ref.shape[1] // 16
    x = x_ref[...].astype(F32)
    for parity, ref in ((0, mine_ref), (1, other_ref)):
        raw = [
            jnp.where(
                core == 0,
                x[:, (2 * j + parity) * n : (2 * j + parity + 1) * n],
                x[:, (2 * j + 1 - parity) * n : (2 * j + 2 - parity) * n],
            )
            for j in range(8)
        ]
        close = [jnp.where(x_lo == 0, raw[i], raw[i + 4]) for i in range(4)]
        away = [jnp.where(x_lo == 0, raw[i + 4], raw[i]) for i in range(4)]
        by_a = roll_blocks(close, y, 1), roll_blocks(away, y, 1)
        for j, (a, dy) in enumerate(TOKEN_ORDER):
            ref[:, j * n : (j + 1) * n] = by_a[a][dy].astype(BF)


def prologue(tokens, gate, up):
    rows, cols = tokens.shape
    half = jax.ShapeDtypeStruct((rows, cols // 2), BF)
    return pl.pallas_call(
        prologue_body,
        out_shape=[
            half,
            half,
            jax.ShapeDtypeStruct((gate.shape[0], 2 * gate.shape[1]), BF),
        ],
        in_specs=[IN_VMEM] * 3,
        out_specs=[IN_VMEM] * 3,
        cost_estimate=SMALL,
        name="prologue",
    )(tokens, gate, up)


def cut_body(x_ref, m0_ref, m1_ref, o0_ref, o1_ref):
    n = m0_ref.shape[0]
    x = x_ref[...].astype(F32)
    parts = [x[i * n : (i + 1) * n] for i in range(4)]
    low = lax.axis_index("x_hi") == 0
    m0_ref[...] = jnp.where(low, parts[0], parts[1]).astype(BF)
    m1_ref[...] = jnp.where(low, parts[1], parts[0]).astype(BF)
    o0_ref[...] = jnp.where(low, parts[2], parts[3]).astype(BF)
    o1_ref[...] = jnp.where(low, parts[3], parts[2]).astype(BF)


def cut_sums(sums):
    rows, cols = sums.shape
    return pl.pallas_call(
        cut_body,
        out_shape=[jax.ShapeDtypeStruct((rows // 4, cols), BF)] * 4,
        in_specs=[IN_VMEM],
        out_specs=[IN_VMEM] * 4,
        cost_estimate=SMALL,
        name="cut_sums",
    )(sums)


def join_body(m0_ref, m1_ref, o0_ref, o1_ref, out_ref):
    x_lo, y, core = (lax.axis_index(a) for a in ("x_lo", "y", "core"))
    n = m0_ref.shape[1] // 8

    def plain(first, second):
        x = first[...].astype(F32) + second[...].astype(F32)
        at = {owner: x[:, j * n : (j + 1) * n] for j, owner in enumerate(INPUT_ORDER)}
        near = roll_blocks([at[0, dy] for dy in range(4)], y, -1)
        far = roll_blocks([at[1, dy] for dy in range(4)], y, -1)
        low = [jnp.where(x_lo == 0, near[i], far[i]) for i in range(4)]
        high = [jnp.where(x_lo == 0, far[i], near[i]) for i in range(4)]
        return low + high

    mine, other = plain(m0_ref, m1_ref), plain(o0_ref, o1_ref)
    for j in range(8):
        out_ref[:, 2 * j * n : (2 * j + 1) * n] = jnp.where(core == 0, mine[j], other[j]).astype(BF)
        out_ref[:, (2 * j + 1) * n : (2 * j + 2) * n] = jnp.where(
            core == 0, other[j], mine[j]
        ).astype(BF)


def join_columns(*parts):
    rows, cols = parts[0].shape
    return pl.pallas_call(
        join_body,
        out_shape=jax.ShapeDtypeStruct((rows, 2 * cols), BF),
        in_specs=[IN_VMEM] * 4,
        out_specs=IN_VMEM,
        cost_estimate=SMALL,
        name="join_columns",
    )(*parts)


def weight_body(scale, start, skip, extra, x_ref, d_ref, *refs):
    out_refs = refs[extra:]
    n = out_refs[0].shape[0]
    acc = lax.dot_general(
        x_ref[:, start : start + skip + n * len(out_refs)],
        d_ref[...],
        (((0,), (0,)), ((), ())),
        preferred_element_type=F32,
    )
    for i, out_ref in enumerate(out_refs):
        out_ref[...] = (acc[skip + i * n : skip + (i + 1) * n] * scale).astype(BF)


def halves_body(a_ref, b_ref, gate_ref, up_ref):
    half = gate_ref.shape[1]
    gate_ref[...] = (a_ref[:, :half].astype(F32) + b_ref[:, :half].astype(F32)).astype(BF)
    up_ref[...] = (a_ref[:, half:].astype(F32) + b_ref[:, half:].astype(F32)).astype(BF)


def add_halves(a, b):
    rows, cols = a.shape
    return pl.pallas_call(
        halves_body,
        out_shape=[jax.ShapeDtypeStruct((rows, cols // 2), BF)] * 2,
        in_specs=[IN_VMEM] * 2,
        out_specs=[IN_VMEM] * 2,
        cost_estimate=SMALL,
        name="add_halves",
    )(a, b)


def merge_body(up_ref, right_ref, down_ref, left_ref, up_out, down_out):
    half = right_ref.shape[1]
    up_out[:, :half] = (up_ref[:, :half].astype(F32) + right_ref[...].astype(F32)).astype(BF)
    up_out[:, half:] = up_ref[:, half:]
    down_out[:, :half] = down_ref[:, :half]
    down_out[:, half:] = (down_ref[:, half:].astype(F32) + left_ref[...].astype(F32)).astype(BF)


def merge(up, right, down, left):
    return pl.pallas_call(
        merge_body,
        out_shape=[jax.ShapeDtypeStruct(up.shape, BF)] * 2,
        in_specs=[IN_VMEM] * 4,
        out_specs=[IN_VMEM] * 2,
        cost_estimate=SMALL,
        name="merge",
    )(up, right, down, left)


def weight_product(x, delta, scale, first, count, n, cost, after=None, tile=768):
    rows, d = x.shape
    cols = delta.shape[1]
    start = first // 128 * 128
    need = min(d, -(-(first + count) // 128) * 128)
    after = [] if after is None else [after]
    return pl.pallas_call(
        functools.partial(weight_body, scale, start, first - start, len(after)),
        out_shape=[jax.ShapeDtypeStruct((n, cols), BF)] * (count // n),
        grid=(cols // tile,),
        in_specs=[
            pl.BlockSpec((rows, need), lambda i: (0, 0)),
            pl.BlockSpec((rows, tile), lambda i: (0, i)),
        ]
        + [pl.BlockSpec(memory_space=pl.ANY)] * len(after),
        out_specs=[pl.BlockSpec((n, tile), lambda i: (0, i))] * (count // n),
        compiler_params=pltpu.CompilerParams(vmem_limit_bytes=VMEM_LIMIT),
        cost_estimate=pl.CostEstimate(
            flops=int(cost), bytes_accessed=1000, transcendentals=0
        ),
        name=f"weight_product_{first}",
    )(x, delta, *after)


def input_body(n, done, *refs):
    blocks, refs = refs[:n], refs[n:]
    (d_ref, out_ref, w, sems), extra = refs[-4:], refs[:-4]
    size, width = blocks[0].shape
    across = w.shape[1] // width

    @pl.when(pl.program_id(0) == 0)
    def _():
        copies = [
            pltpu.make_async_copy(
                b,
                w.at[pl.ds(i // across * size, size), pl.ds(i % across * width, width)],
                sems.at[i],
            )
            for i, b in enumerate(blocks)
        ]
        for c in copies:
            c.start()
        for c in copies:
            c.wait()

    at = 0
    for ref in extra if done else ():
        out_ref[:, at : at + ref.shape[1]] = ref[...]
        at += ref.shape[1]
    out_ref[:, done:] = lax.dot_general(
        d_ref[...], w[...], (((1,), (1,)), ((), ())), preferred_element_type=F32
    ).astype(BF)


def input_product(delta, blocks, before=(), tile=352):
    rows, cols = delta.shape
    n = len(blocks)
    done = sum(b.shape[1] for b in before)
    size = n * blocks[0].size // cols
    d = done + size
    return pl.pallas_call(
        functools.partial(input_body, n, done),
        out_shape=jax.ShapeDtypeStruct((rows, d), BF),
        grid=(rows // tile,),
        in_specs=[pl.BlockSpec(memory_space=pl.ANY)] * n
        + [pl.BlockSpec((tile, b.shape[1]), lambda i: (i, 0)) for b in before]
        + [pl.BlockSpec((tile, cols), lambda i: (i, 0))],
        out_specs=pl.BlockSpec((tile, d), lambda i: (i, 0)),
        scratch_shapes=[pltpu.VMEM((size, cols), BF), pltpu.SemaphoreType.DMA((n,))],
        compiler_params=pltpu.CompilerParams(vmem_limit_bytes=40 * 1024 * 1024),
        cost_estimate=SMALL,
        name=f"input_product_{n}",
    )(*blocks, *before, delta)


def gather_weights(w, after, then):
    half = w.shape[1] // 2
    below, above, far = shift(w, "y", 1), shift(w, "y", -1), shift(w, "x_lo", 1)
    below, above, far, after = lax.optimization_barrier((below, above, far, after))
    far_below, far_above = shift(below, "x_lo", 1), shift(far, "y", -1)
    across = shift(below, "y", 1)
    then = then(after, [w, far, above, below])
    far_below, far_above, then = lax.optimization_barrier((far_below, far_above, then))
    last = [shift(far_below[:, :half], "y", 1), shift(far_above[:, half:], "y", -1)]
    return [across, far_above, far_below], last, then


def scatter_grads(blocks):
    across, far_up, far_down, far, far_own, up, down, own = blocks
    across = shift(across, "x_lo", 1)
    far_right, far_left = shift(far_up, "y", 1), shift(far_down, "y", -1)
    across, far_right, far_left = lax.optimization_barrier((across, far_right, far_left))
    right, left = add_halves(far, across)
    right, left = shift(right, "y", 1), shift(left, "y", -1)
    far_own = shift(add(far_own, far_left, far_right), "x_lo", 1)
    up, down = merge(up, right, down, left)
    return own, shift(up, "y", 1), shift(down, "y", -1), far_own


def per_device(tokens, gate_pre, up_pre, cotangent, gate_weight, up_weight):
    x_hi = lax.axis_index("x_hi")
    scale = 1.0 / math.sqrt(gate_pre.shape[0] * 16)
    rows, hidden = tokens.shape[0], gate_weight.shape[1]
    owned = gate_weight.shape[0]

    keep, give, w = prologue(tokens, gate_weight, up_weight)
    pair = jnp.stack([keep, shift(give, "core", 1)])
    far = shift(pair, "x_hi", 1)
    block = jnp.where(
        x_hi == 0, jnp.concatenate([pair, far], 1), jnp.concatenate([far, pair], 1)
    )
    gate_pre, block = lax.optimization_barrier((gate_pre, block))
    x = lax.all_gather(block, "z", axis=0, tiled=True).reshape(-1, keep.shape[1])
    mine = make_deltas(gate_pre, up_pre, cotangent)

    def first_part(mine, blocks):
        other = shift(mine, "core", 1)
        delta = jnp.stack([a.reshape(8, 2 * rows, -1) for a in (mine, other)], 1)
        delta = delta.reshape(-1, 2 * hidden)
        return delta, input_product(delta, blocks)

    middle, last, (delta, part) = gather_weights(w, mine, first_part)
    part = [part, input_product(delta, middle)]
    part = input_product(delta, last, part)
    sums = lax.psum_scatter(part, "z", scatter_dimension=0, tiled=True)

    first = weight_product(x, delta, scale, 0, 3 * owned, owned, 1e3, tile=hidden)
    rest = weight_product(
        x, delta, scale, 3 * owned, 5 * owned, owned, REST_FLOPS, mark("sent", *first)
    )
    terms = scatter_grads(first + rest)

    here, there, here_other, there_other = cut_sums(sums)
    parts = [here, shift(there, "x_hi", 1), both_flipped(there_other)]
    parts.append(shift(here_other, "core", 1))
    grads = add(*terms)
    grads, *parts = lax.optimization_barrier((grads, *parts))
    input_grad = join_columns(*parts)
    return input_grad, grads[:, :hidden], grads[:, hidden:]


def solution(mesh):
    fine = Mesh(mesh.devices.reshape(8, 2, 2, 4, 2), ("z", "x_hi", "x_lo", "y", "core"))
    fsdp, fsdpt = ("z", "x_hi"), ("x_lo", "y", "core")
    both = P(fsdpt, fsdp)
    return jax.shard_map(
        per_device,
        mesh=fine,
        in_specs=(P(fsdpt + fsdp, None), both, both, both, both, both),
        out_specs=(P(fsdpt + fsdp, None), both, both),
        check_vma=False,
    )
```

```python
import functools
import math

import jax
import jax.numpy as jnp
from jax import lax
from jax.experimental import pallas as pl
from jax.experimental.pallas import tpu as pltpu
from jax.sharding import Mesh, PartitionSpec as P

BF = jnp.bfloat16
F32 = jnp.float32
VMEM_LIMIT = 56 * 1024 * 1024
IN_VMEM = pl.BlockSpec(memory_space=pltpu.VMEM)
SMALL = pl.CostEstimate(flops=1000, bytes_accessed=1000, transcendentals=0)
MARK_FLOPS = 1e12
DELTA_FLOPS = 1e11
REST_FLOPS = 1e11


def shift(x, axis, k):
    n = lax.axis_size(axis)
    return lax.ppermute(x, axis, [(i, (i + k) % n) for i in range(n)])


def both_flipped(x):
    return lax.ppermute(x, ("x_hi", "core"), [(i, 3 - i) for i in range(4)])


def add(*xs):
    total = xs[0].astype(F32)
    for x in xs[1:]:
        total = total + x.astype(F32)
    return total.astype(BF)


def delta_body(g_ref, u_ref, c_ref, out_ref):
    g = g_ref[...].astype(F32)
    u = u_ref[...].astype(F32)
    c = c_ref[...].astype(F32)
    kappa = math.sqrt(2.0 / math.pi)
    g2 = g * g
    tangent = jnp.tanh(kappa * (g + 0.044715 * g2 * g))
    half = 0.5 * (1.0 + tangent)
    act = g * half
    slope = half + 0.5 * g * (1.0 - tangent * tangent) * kappa * (1.0 + 3.0 * 0.044715 * g2)
    n = g.shape[1]
    out_ref[:, :n] = (c * u * slope).astype(BF)
    out_ref[:, n:] = (c * act).astype(BF)


def make_deltas(g, u, c, tile=176):
    rows, cols = g.shape
    spec = pl.BlockSpec((tile, cols), lambda i: (i, 0))
    return pl.pallas_call(
        delta_body,
        out_shape=jax.ShapeDtypeStruct((rows, 2 * cols), BF),
        grid=(rows // tile,),
        in_specs=[spec] * 3,
        out_specs=pl.BlockSpec((tile, 2 * cols), lambda i: (i, 0)),
        compiler_params=pltpu.CompilerParams(vmem_limit_bytes=VMEM_LIMIT),
        cost_estimate=pl.CostEstimate(flops=int(DELTA_FLOPS), bytes_accessed=1000, transcendentals=0),
        name="deltas",
    )(g, u, c)


def mark_body(*refs):
    refs[-1][...] = jnp.zeros_like(refs[-1])


def mark(name, *after):
    return pl.pallas_call(
        mark_body,
        out_shape=jax.ShapeDtypeStruct((8, 128), F32),
        in_specs=[pl.BlockSpec(memory_space=pl.ANY)] * len(after),
        out_specs=IN_VMEM,
        cost_estimate=pl.CostEstimate(
            flops=int(MARK_FLOPS), bytes_accessed=1000, transcendentals=0
        ),
        name=name,
    )(*after)


INPUT_ORDER = ((0, 0), (1, 0), (0, 1), (0, 3), (0, 2), (1, 1), (1, 3), (1, 2))
TOKEN_ORDER = ((1, 2), (1, 1), (1, 3), (0, 2), (1, 0), (0, 1), (0, 3), (0, 0))


def roll_blocks(blocks, y, sign):
    one = [jnp.where(y % 2 == 1, blocks[(i + sign) % 4], blocks[i]) for i in range(4)]
    return [jnp.where(y >= 2, one[(i + 2) % 4], one[i]) for i in range(4)]


def prologue_body(x_ref, g_ref, u_ref, mine_ref, other_ref, w_ref):
    hidden = g_ref.shape[1]
    w_ref[:, :hidden] = g_ref[...]
    w_ref[:, hidden:] = u_ref[...]
    x_lo, y, core = (lax.axis_index(a) for a in ("x_lo", "y", "core"))
    n = x_ref.shape[1] // 16
    x = x_ref[...].astype(F32)
    for parity, ref in ((0, mine_ref), (1, other_ref)):
        raw = [
            jnp.where(
                core == 0,
                x[:, (2 * j + parity) * n : (2 * j + parity + 1) * n],
                x[:, (2 * j + 1 - parity) * n : (2 * j + 2 - parity) * n],
            )
            for j in range(8)
        ]
        close = [jnp.where(x_lo == 0, raw[i], raw[i + 4]) for i in range(4)]
        away = [jnp.where(x_lo == 0, raw[i + 4], raw[i]) for i in range(4)]
        by_a = roll_blocks(close, y, 1), roll_blocks(away, y, 1)
        for j, (a, dy) in enumerate(TOKEN_ORDER):
            ref[:, j * n : (j + 1) * n] = by_a[a][dy].astype(BF)


def prologue(tokens, gate, up):
    rows, cols = tokens.shape
    half = jax.ShapeDtypeStruct((rows, cols // 2), BF)
    return pl.pallas_call(
        prologue_body,
        out_shape=[
            half,
            half,
            jax.ShapeDtypeStruct((gate.shape[0], 2 * gate.shape[1]), BF),
        ],
        in_specs=[IN_VMEM] * 3,
        out_specs=[IN_VMEM] * 3,
        cost_estimate=SMALL,
        name="prologue",
    )(tokens, gate, up)


def cut_body(x_ref, m0_ref, m1_ref, o0_ref, o1_ref):
    n = m0_ref.shape[0]
    x = x_ref[...].astype(F32)
    parts = [x[i * n : (i + 1) * n] for i in range(4)]
    low = lax.axis_index("x_hi") == 0
    m0_ref[...] = jnp.where(low, parts[0], parts[1]).astype(BF)
    m1_ref[...] = jnp.where(low, parts[1], parts[0]).astype(BF)
    o0_ref[...] = jnp.where(low, parts[2], parts[3]).astype(BF)
    o1_ref[...] = jnp.where(low, parts[3], parts[2]).astype(BF)


def cut_sums(sums):
    rows, cols = sums.shape
    return pl.pallas_call(
        cut_body,
        out_shape=[jax.ShapeDtypeStruct((rows // 4, cols), BF)] * 4,
        in_specs=[IN_VMEM],
        out_specs=[IN_VMEM] * 4,
        cost_estimate=SMALL,
        name="cut_sums",
    )(sums)


def join_body(m0_ref, m1_ref, o0_ref, o1_ref, out_ref):
    x_lo, y, core = (lax.axis_index(a) for a in ("x_lo", "y", "core"))
    n = m0_ref.shape[1] // 8

    def plain(first, second):
        x = first[...].astype(F32) + second[...].astype(F32)
        at = {owner: x[:, j * n : (j + 1) * n] for j, owner in enumerate(INPUT_ORDER)}
        near = roll_blocks([at[0, dy] for dy in range(4)], y, -1)
        far = roll_blocks([at[1, dy] for dy in range(4)], y, -1)
        low = [jnp.where(x_lo == 0, near[i], far[i]) for i in range(4)]
        high = [jnp.where(x_lo == 0, far[i], near[i]) for i in range(4)]
        return low + high

    mine, other = plain(m0_ref, m1_ref), plain(o0_ref, o1_ref)
    for j in range(8):
        out_ref[:, 2 * j * n : (2 * j + 1) * n] = jnp.where(core == 0, mine[j], other[j]).astype(BF)
        out_ref[:, (2 * j + 1) * n : (2 * j + 2) * n] = jnp.where(
            core == 0, other[j], mine[j]
        ).astype(BF)


def join_columns(*parts):
    rows, cols = parts[0].shape
    return pl.pallas_call(
        join_body,
        out_shape=jax.ShapeDtypeStruct((rows, 2 * cols), BF),
        in_specs=[IN_VMEM] * 4,
        out_specs=IN_VMEM,
        cost_estimate=SMALL,
        name="join_columns",
    )(*parts)


def weight_body(scale, start, skip, extra, x_ref, d_ref, *refs):
    out_refs = refs[extra:]
    n = out_refs[0].shape[0]
    acc = lax.dot_general(
        x_ref[:, start : start + skip + n * len(out_refs)],
        d_ref[...],
        (((0,), (0,)), ((), ())),
        preferred_element_type=F32,
    )
    for i, out_ref in enumerate(out_refs):
        out_ref[...] = (acc[skip + i * n : skip + (i + 1) * n] * scale).astype(BF)


def halves_body(a_ref, b_ref, gate_ref, up_ref):
    half = gate_ref.shape[1]
    gate_ref[...] = (a_ref[:, :half].astype(F32) + b_ref[:, :half].astype(F32)).astype(BF)
    up_ref[...] = (a_ref[:, half:].astype(F32) + b_ref[:, half:].astype(F32)).astype(BF)


def add_halves(a, b):
    rows, cols = a.shape
    return pl.pallas_call(
        halves_body,
        out_shape=[jax.ShapeDtypeStruct((rows, cols // 2), BF)] * 2,
        in_specs=[IN_VMEM] * 2,
        out_specs=[IN_VMEM] * 2,
        cost_estimate=SMALL,
        name="add_halves",
    )(a, b)


def merge_body(up_ref, right_ref, down_ref, left_ref, up_out, down_out):
    half = right_ref.shape[1]
    up_out[:, :half] = (up_ref[:, :half].astype(F32) + right_ref[...].astype(F32)).astype(BF)
    up_out[:, half:] = up_ref[:, half:]
    down_out[:, :half] = down_ref[:, :half]
    down_out[:, half:] = (down_ref[:, half:].astype(F32) + left_ref[...].astype(F32)).astype(BF)


def merge(up, right, down, left):
    return pl.pallas_call(
        merge_body,
        out_shape=[jax.ShapeDtypeStruct(up.shape, BF)] * 2,
        in_specs=[IN_VMEM] * 4,
        out_specs=[IN_VMEM] * 2,
        cost_estimate=SMALL,
        name="merge",
    )(up, right, down, left)


def weight_product(x, delta, scale, first, count, n, cost, after=None, tile=768):
    rows, d = x.shape
    cols = delta.shape[1]
    start = first // 128 * 128
    need = min(d, -(-(first + count) // 128) * 128)
    after = [] if after is None else [after]
    return pl.pallas_call(
        functools.partial(weight_body, scale, start, first - start, len(after)),
        out_shape=[jax.ShapeDtypeStruct((n, cols), BF)] * (count // n),
        grid=(cols // tile,),
        in_specs=[
            pl.BlockSpec((rows, need), lambda i: (0, 0)),
            pl.BlockSpec((rows, tile), lambda i: (0, i)),
        ]
        + [pl.BlockSpec(memory_space=pl.ANY)] * len(after),
        out_specs=[pl.BlockSpec((n, tile), lambda i: (0, i))] * (count // n),
        compiler_params=pltpu.CompilerParams(vmem_limit_bytes=VMEM_LIMIT),
        cost_estimate=pl.CostEstimate(
            flops=int(cost), bytes_accessed=1000, transcendentals=0
        ),
        name=f"weight_product_{first}",
    )(x, delta, *after)


def input_body(n, done, *refs):
    blocks, refs = refs[:n], refs[n:]
    (d_ref, out_ref, w, sems), extra = refs[-4:], refs[:-4]
    size, width = blocks[0].shape
    across = w.shape[1] // width

    @pl.when(pl.program_id(0) == 0)
    def _():
        copies = [
            pltpu.make_async_copy(
                b,
                w.at[pl.ds(i // across * size, size), pl.ds(i % across * width, width)],
                sems.at[i],
            )
            for i, b in enumerate(blocks)
        ]
        for c in copies:
            c.start()
        for c in copies:
            c.wait()

    at = 0
    for ref in extra if done else ():
        out_ref[:, at : at + ref.shape[1]] = ref[...]
        at += ref.shape[1]
    out_ref[:, done:] = lax.dot_general(
        d_ref[...], w[...], (((1,), (1,)), ((), ())), preferred_element_type=F32
    ).astype(BF)


def input_product(delta, blocks, before=(), tile=352):
    rows, cols = delta.shape
    n = len(blocks)
    done = sum(b.shape[1] for b in before)
    size = n * blocks[0].size // cols
    d = done + size
    return pl.pallas_call(
        functools.partial(input_body, n, done),
        out_shape=jax.ShapeDtypeStruct((rows, d), BF),
        grid=(rows // tile,),
        in_specs=[pl.BlockSpec(memory_space=pl.ANY)] * n
        + [pl.BlockSpec((tile, b.shape[1]), lambda i: (i, 0)) for b in before]
        + [pl.BlockSpec((tile, cols), lambda i: (i, 0))],
        out_specs=pl.BlockSpec((tile, d), lambda i: (i, 0)),
        scratch_shapes=[pltpu.VMEM((size, cols), BF), pltpu.SemaphoreType.DMA((n,))],
        compiler_params=pltpu.CompilerParams(vmem_limit_bytes=40 * 1024 * 1024),
        cost_estimate=SMALL,
        name=f"input_product_{n}",
    )(*blocks, *before, delta)


def gather_weights(w, after, then):
    half = w.shape[1] // 2
    below, above, far = shift(w, "y", 1), shift(w, "y", -1), shift(w, "x_lo", 1)
    below, above, far, after = lax.optimization_barrier((below, above, far, after))
    far_below, far_above = shift(below, "x_lo", 1), shift(far, "y", -1)
    across = shift(below, "y", 1)
    then = then(after, [w, far, above, below])
    far_below, far_above, then = lax.optimization_barrier((far_below, far_above, then))
    last = [shift(far_below[:, :half], "y", 1), shift(far_above[:, half:], "y", -1)]
    return [across, far_above, far_below], last, then


def scatter_grads(blocks):
    across, far_up, far_down, far, far_own, up, down, own = blocks
    across = shift(across, "x_lo", 1)
    far_right, far_left = shift(far_up, "y", 1), shift(far_down, "y", -1)
    right, left = add_halves(far, across)
    right, left = shift(right, "y", 1), shift(left, "y", -1)
    far_own = shift(add(far_own, far_left, far_right), "x_lo", 1)
    up, down = merge(up, right, down, left)
    return own, shift(up, "y", 1), shift(down, "y", -1), far_own


def per_device(tokens, gate_pre, up_pre, cotangent, gate_weight, up_weight):
    x_hi = lax.axis_index("x_hi")
    scale = 1.0 / math.sqrt(gate_pre.shape[0] * 16)
    rows, hidden = tokens.shape[0], gate_weight.shape[1]
    owned = gate_weight.shape[0]

    keep, give, w = prologue(tokens, gate_weight, up_weight)
    pair = jnp.stack([keep, shift(give, "core", 1)])
    far = shift(pair, "x_hi", 1)
    block = jnp.where(
        x_hi == 0, jnp.concatenate([pair, far], 1), jnp.concatenate([far, pair], 1)
    )
    gate_pre, block = lax.optimization_barrier((gate_pre, block))
    x = lax.all_gather(block, "z", axis=0, tiled=True).reshape(-1, keep.shape[1])
    mine = make_deltas(gate_pre, up_pre, cotangent)

    def first_part(mine, blocks):
        other = shift(mine, "core", 1)
        delta = jnp.stack([a.reshape(8, 2 * rows, -1) for a in (mine, other)], 1)
        delta = delta.reshape(-1, 2 * hidden)
        return delta, input_product(delta, blocks)

    middle, last, (delta, part) = gather_weights(w, mine, first_part)
    part = [part, input_product(delta, middle)]
    part = input_product(delta, last, part)
    sums = lax.psum_scatter(part, "z", scatter_dimension=0, tiled=True)

    first = weight_product(x, delta, scale, 0, 3 * owned, owned, 1e3, tile=hidden)
    rest = weight_product(
        x, delta, scale, 3 * owned, 5 * owned, owned, REST_FLOPS, mark("sent", *first)
    )
    terms = scatter_grads(first + rest)

    here, there, here_other, there_other = cut_sums(sums)
    parts = [here, shift(there, "x_hi", 1), both_flipped(there_other)]
    parts.append(shift(here_other, "core", 1))
    input_grad = join_columns(*parts)
    input_grad, *terms = lax.optimization_barrier((input_grad, *terms))
    gate_grad = add(*(t[:, :hidden] for t in terms))
    up_grad = add(*(t[:, hidden:] for t in terms))
    return input_grad, gate_grad, up_grad


def solution(mesh):
    fine = Mesh(mesh.devices.reshape(8, 2, 2, 4, 2), ("z", "x_hi", "x_lo", "y", "core"))
    fsdp, fsdpt = ("z", "x_hi"), ("x_lo", "y", "core")
    both = P(fsdpt, fsdp)
    return jax.shard_map(
        per_device,
        mesh=fine,
        in_specs=(P(fsdpt + fsdp, None), both, both, both, both, both),
        out_specs=(P(fsdpt + fsdp, None), both, both),
        check_vma=False,
    )
```

```python
import functools
import math

import jax
import jax.numpy as jnp
from jax import lax
from jax.experimental import pallas as pl
from jax.experimental.pallas import tpu as pltpu
from jax.sharding import Mesh, PartitionSpec as P

BF = jnp.bfloat16
F32 = jnp.float32
VMEM_LIMIT = 56 * 1024 * 1024
IN_VMEM = pl.BlockSpec(memory_space=pltpu.VMEM)
SMALL = pl.CostEstimate(flops=1000, bytes_accessed=1000, transcendentals=0)
MARK_FLOPS = 1e12
DELTA_FLOPS = 1e11
REST_FLOPS = 1e11


def shift(x, axis, k):
    n = lax.axis_size(axis)
    return lax.ppermute(x, axis, [(i, (i + k) % n) for i in range(n)])


def both_flipped(x):
    return lax.ppermute(x, ("x_hi", "core"), [(i, 3 - i) for i in range(4)])


def add(*xs):
    total = xs[0].astype(F32)
    for x in xs[1:]:
        total = total + x.astype(F32)
    return total.astype(BF)


def delta_body(g_ref, u_ref, c_ref, out_ref):
    g = g_ref[...].astype(F32)
    u = u_ref[...].astype(F32)
    c = c_ref[...].astype(F32)
    kappa = math.sqrt(2.0 / math.pi)
    g2 = g * g
    tangent = jnp.tanh(kappa * (g + 0.044715 * g2 * g))
    half = 0.5 * (1.0 + tangent)
    act = g * half
    slope = half + 0.5 * g * (1.0 - tangent * tangent) * kappa * (1.0 + 3.0 * 0.044715 * g2)
    n = g.shape[1]
    out_ref[:, :n] = (c * u * slope).astype(BF)
    out_ref[:, n:] = (c * act).astype(BF)


def make_deltas(g, u, c, tile=176):
    rows, cols = g.shape
    spec = pl.BlockSpec((tile, cols), lambda i: (i, 0))
    return pl.pallas_call(
        delta_body,
        out_shape=jax.ShapeDtypeStruct((rows, 2 * cols), BF),
        grid=(rows // tile,),
        in_specs=[spec] * 3,
        out_specs=pl.BlockSpec((tile, 2 * cols), lambda i: (i, 0)),
        compiler_params=pltpu.CompilerParams(vmem_limit_bytes=VMEM_LIMIT),
        cost_estimate=pl.CostEstimate(flops=int(DELTA_FLOPS), bytes_accessed=1000, transcendentals=0),
        name="deltas",
    )(g, u, c)


def mark_body(*refs):
    refs[-1][...] = jnp.zeros_like(refs[-1])


def mark(name, *after):
    return pl.pallas_call(
        mark_body,
        out_shape=jax.ShapeDtypeStruct((8, 128), F32),
        in_specs=[pl.BlockSpec(memory_space=pl.ANY)] * len(after),
        out_specs=IN_VMEM,
        cost_estimate=pl.CostEstimate(
            flops=int(MARK_FLOPS), bytes_accessed=1000, transcendentals=0
        ),
        name=name,
    )(*after)


INPUT_ORDER = ((0, 0), (1, 0), (0, 1), (0, 3), (0, 2), (1, 1), (1, 3), (1, 2))
TOKEN_ORDER = ((1, 2), (1, 1), (1, 3), (0, 2), (1, 0), (0, 1), (0, 3), (0, 0))


def roll_blocks(blocks, y, sign):
    one = [jnp.where(y % 2 == 1, blocks[(i + sign) % 4], blocks[i]) for i in range(4)]
    return [jnp.where(y >= 2, one[(i + 2) % 4], one[i]) for i in range(4)]


def prologue_body(x_ref, g_ref, u_ref, mine_ref, other_ref, w_ref):
    hidden = g_ref.shape[1]
    w_ref[:, :hidden] = g_ref[...]
    w_ref[:, hidden:] = u_ref[...]
    x_lo, y, core = (lax.axis_index(a) for a in ("x_lo", "y", "core"))
    n = x_ref.shape[1] // 16
    x = x_ref[...].astype(F32)
    for parity, ref in ((0, mine_ref), (1, other_ref)):
        raw = [
            jnp.where(
                core == 0,
                x[:, (2 * j + parity) * n : (2 * j + parity + 1) * n],
                x[:, (2 * j + 1 - parity) * n : (2 * j + 2 - parity) * n],
            )
            for j in range(8)
        ]
        close = [jnp.where(x_lo == 0, raw[i], raw[i + 4]) for i in range(4)]
        away = [jnp.where(x_lo == 0, raw[i + 4], raw[i]) for i in range(4)]
        by_a = roll_blocks(close, y, 1), roll_blocks(away, y, 1)
        for j, (a, dy) in enumerate(TOKEN_ORDER):
            ref[:, j * n : (j + 1) * n] = by_a[a][dy].astype(BF)


def prologue(tokens, gate, up):
    rows, cols = tokens.shape
    half = jax.ShapeDtypeStruct((rows, cols // 2), BF)
    return pl.pallas_call(
        prologue_body,
        out_shape=[
            half,
            half,
            jax.ShapeDtypeStruct((gate.shape[0], 2 * gate.shape[1]), BF),
        ],
        in_specs=[IN_VMEM] * 3,
        out_specs=[IN_VMEM] * 3,
        cost_estimate=SMALL,
        name="prologue",
    )(tokens, gate, up)


def cut_body(x_ref, m0_ref, m1_ref, o0_ref, o1_ref):
    n = m0_ref.shape[0]
    x = x_ref[...].astype(F32)
    parts = [x[i * n : (i + 1) * n] for i in range(4)]
    low = lax.axis_index("x_hi") == 0
    m0_ref[...] = jnp.where(low, parts[0], parts[1]).astype(BF)
    m1_ref[...] = jnp.where(low, parts[1], parts[0]).astype(BF)
    o0_ref[...] = jnp.where(low, parts[2], parts[3]).astype(BF)
    o1_ref[...] = jnp.where(low, parts[3], parts[2]).astype(BF)


def cut_sums(sums):
    rows, cols = sums.shape
    return pl.pallas_call(
        cut_body,
        out_shape=[jax.ShapeDtypeStruct((rows // 4, cols), BF)] * 4,
        in_specs=[IN_VMEM],
        out_specs=[IN_VMEM] * 4,
        cost_estimate=SMALL,
        name="cut_sums",
    )(sums)


def join_body(m0_ref, m1_ref, o0_ref, o1_ref, out_ref):
    x_lo, y, core = (lax.axis_index(a) for a in ("x_lo", "y", "core"))
    n = m0_ref.shape[1] // 8

    def plain(first, second):
        x = first[...].astype(F32) + second[...].astype(F32)
        at = {owner: x[:, j * n : (j + 1) * n] for j, owner in enumerate(INPUT_ORDER)}
        near = roll_blocks([at[0, dy] for dy in range(4)], y, -1)
        far = roll_blocks([at[1, dy] for dy in range(4)], y, -1)
        low = [jnp.where(x_lo == 0, near[i], far[i]) for i in range(4)]
        high = [jnp.where(x_lo == 0, far[i], near[i]) for i in range(4)]
        return low + high

    mine, other = plain(m0_ref, m1_ref), plain(o0_ref, o1_ref)
    for j in range(8):
        out_ref[:, 2 * j * n : (2 * j + 1) * n] = jnp.where(core == 0, mine[j], other[j]).astype(BF)
        out_ref[:, (2 * j + 1) * n : (2 * j + 2) * n] = jnp.where(
            core == 0, other[j], mine[j]
        ).astype(BF)


def join_columns(*parts):
    rows, cols = parts[0].shape
    return pl.pallas_call(
        join_body,
        out_shape=jax.ShapeDtypeStruct((rows, 2 * cols), BF),
        in_specs=[IN_VMEM] * 4,
        out_specs=IN_VMEM,
        cost_estimate=SMALL,
        name="join_columns",
    )(*parts)


def weight_body(scale, start, skip, extra, x_ref, d_ref, *refs):
    out_refs = refs[extra:]
    n = out_refs[0].shape[0]
    acc = lax.dot_general(
        x_ref[:, start : start + skip + n * len(out_refs)],
        d_ref[...],
        (((0,), (0,)), ((), ())),
        preferred_element_type=F32,
    )
    for i, out_ref in enumerate(out_refs):
        out_ref[...] = (acc[skip + i * n : skip + (i + 1) * n] * scale).astype(BF)


def halves_body(a_ref, b_ref, gate_ref, up_ref):
    half = gate_ref.shape[1]
    gate_ref[...] = (a_ref[:, :half].astype(F32) + b_ref[:, :half].astype(F32)).astype(BF)
    up_ref[...] = (a_ref[:, half:].astype(F32) + b_ref[:, half:].astype(F32)).astype(BF)


def add_halves(a, b):
    rows, cols = a.shape
    return pl.pallas_call(
        halves_body,
        out_shape=[jax.ShapeDtypeStruct((rows, cols // 2), BF)] * 2,
        in_specs=[IN_VMEM] * 2,
        out_specs=[IN_VMEM] * 2,
        cost_estimate=SMALL,
        name="add_halves",
    )(a, b)


def merge_body(up_ref, right_ref, down_ref, left_ref, up_out, down_out):
    half = right_ref.shape[1]
    up_out[:, :half] = (up_ref[:, :half].astype(F32) + right_ref[...].astype(F32)).astype(BF)
    up_out[:, half:] = up_ref[:, half:]
    down_out[:, :half] = down_ref[:, :half]
    down_out[:, half:] = (down_ref[:, half:].astype(F32) + left_ref[...].astype(F32)).astype(BF)


def merge(up, right, down, left):
    return pl.pallas_call(
        merge_body,
        out_shape=[jax.ShapeDtypeStruct(up.shape, BF)] * 2,
        in_specs=[IN_VMEM] * 4,
        out_specs=[IN_VMEM] * 2,
        cost_estimate=SMALL,
        name="merge",
    )(up, right, down, left)


def weight_product(x, delta, scale, first, count, n, cost, after=None, tile=768):
    rows, d = x.shape
    cols = delta.shape[1]
    start = first // 128 * 128
    need = min(d, -(-(first + count) // 128) * 128)
    after = [] if after is None else [after]
    return pl.pallas_call(
        functools.partial(weight_body, scale, start, first - start, len(after)),
        out_shape=[jax.ShapeDtypeStruct((n, cols), BF)] * (count // n),
        grid=(cols // tile,),
        in_specs=[
            pl.BlockSpec((rows, need), lambda i: (0, 0)),
            pl.BlockSpec((rows, tile), lambda i: (0, i)),
        ]
        + [pl.BlockSpec(memory_space=pl.ANY)] * len(after),
        out_specs=[pl.BlockSpec((n, tile), lambda i: (0, i))] * (count // n),
        compiler_params=pltpu.CompilerParams(vmem_limit_bytes=VMEM_LIMIT),
        cost_estimate=pl.CostEstimate(
            flops=int(cost), bytes_accessed=1000, transcendentals=0
        ),
        name=f"weight_product_{first}",
    )(x, delta, *after)


def input_body(n, done, *refs):
    blocks, refs = refs[:n], refs[n:]
    (d_ref, out_ref, w, sems), extra = refs[-4:], refs[:-4]
    size, width = blocks[0].shape
    across = w.shape[1] // width

    @pl.when(pl.program_id(0) == 0)
    def _():
        copies = [
            pltpu.make_async_copy(
                b,
                w.at[pl.ds(i // across * size, size), pl.ds(i % across * width, width)],
                sems.at[i],
            )
            for i, b in enumerate(blocks)
        ]
        for c in copies:
            c.start()
        for c in copies:
            c.wait()

    at = 0
    for ref in extra if done else ():
        out_ref[:, at : at + ref.shape[1]] = ref[...]
        at += ref.shape[1]
    out_ref[:, done:] = lax.dot_general(
        d_ref[...], w[...], (((1,), (1,)), ((), ())), preferred_element_type=F32
    ).astype(BF)


def input_product(delta, blocks, before=(), tile=352):
    rows, cols = delta.shape
    n = len(blocks)
    done = sum(b.shape[1] for b in before)
    size = n * blocks[0].size // cols
    d = done + size
    return pl.pallas_call(
        functools.partial(input_body, n, done),
        out_shape=jax.ShapeDtypeStruct((rows, d), BF),
        grid=(rows // tile,),
        in_specs=[pl.BlockSpec(memory_space=pl.ANY)] * n
        + [pl.BlockSpec((tile, b.shape[1]), lambda i: (i, 0)) for b in before]
        + [pl.BlockSpec((tile, cols), lambda i: (i, 0))],
        out_specs=pl.BlockSpec((tile, d), lambda i: (i, 0)),
        scratch_shapes=[pltpu.VMEM((size, cols), BF), pltpu.SemaphoreType.DMA((n,))],
        compiler_params=pltpu.CompilerParams(vmem_limit_bytes=40 * 1024 * 1024),
        cost_estimate=SMALL,
        name=f"input_product_{n}",
    )(*blocks, *before, delta)


def gather_weights(w, after, then):
    half = w.shape[1] // 2
    below, above, far = shift(w, "y", 1), shift(w, "y", -1), shift(w, "x_lo", 1)
    below, above, far, after = lax.optimization_barrier((below, above, far, after))
    far_below, far_above = shift(below, "x_lo", 1), shift(far, "y", -1)
    across = shift(below, "y", 1)
    then = then(after, [w, far, above, below])
    far_below, far_above, then = lax.optimization_barrier((far_below, far_above, then))
    last = [shift(far_below[:, :half], "y", 1), shift(far_above[:, half:], "y", -1)]
    return [across, far_above, far_below], last, then


def scatter_grads(blocks):
    across, far_up, far_down, far, far_own, up, down, own = blocks
    across = shift(across, "x_lo", 1)
    far_right, far_left = shift(far_up, "y", 1), shift(far_down, "y", -1)
    right, left = add_halves(far, across)
    right, left = shift(right, "y", 1), shift(left, "y", -1)
    far_own = shift(add(far_own, far_left, far_right), "x_lo", 1)
    up, down = merge(up, right, down, left)
    return own, shift(up, "y", 1), shift(down, "y", -1), far_own


def per_device(tokens, gate_pre, up_pre, cotangent, gate_weight, up_weight):
    x_hi = lax.axis_index("x_hi")
    scale = 1.0 / math.sqrt(gate_pre.shape[0] * 16)
    rows, hidden = tokens.shape[0], gate_weight.shape[1]
    owned = gate_weight.shape[0]

    keep, give, w = prologue(tokens, gate_weight, up_weight)
    pair = jnp.stack([keep, shift(give, "core", 1)])
    far = shift(pair, "x_hi", 1)
    block = jnp.where(
        x_hi == 0, jnp.concatenate([pair, far], 1), jnp.concatenate([far, pair], 1)
    )
    gate_pre, block = lax.optimization_barrier((gate_pre, block))
    x = lax.all_gather(block, "z", axis=0, tiled=True).reshape(-1, keep.shape[1])
    mine = make_deltas(gate_pre, up_pre, cotangent)

    def first_part(mine, blocks):
        other = shift(mine, "core", 1)
        delta = jnp.stack([a.reshape(8, 2 * rows, -1) for a in (mine, other)], 1)
        delta = delta.reshape(-1, 2 * hidden)
        return delta, input_product(delta, blocks)

    middle, last, (delta, part) = gather_weights(w, mine, first_part)
    part = [part, input_product(delta, middle)]
    part = input_product(delta, last, part)
    sums = lax.psum_scatter(part, "z", scatter_dimension=0, tiled=True)

    first = weight_product(x, delta, scale, 0, 3 * owned, owned, 1e3, tile=hidden)
    rest = weight_product(
        x, delta, scale, 3 * owned, 5 * owned, owned, REST_FLOPS, mark("sent", *first)
    )
    terms = scatter_grads(first + rest)

    here, there, here_other, there_other = cut_sums(sums)
    parts = [here, shift(there, "x_hi", 1), both_flipped(there_other)]
    parts.append(shift(here_other, "core", 1))
    gate_grad = add(*(t[:, :hidden] for t in terms))
    up_grad = add(*(t[:, hidden:] for t in terms))
    gate_grad, up_grad, *parts = lax.optimization_barrier((gate_grad, up_grad, *parts))
    return join_columns(*parts), gate_grad, up_grad


def solution(mesh):
    fine = Mesh(mesh.devices.reshape(8, 2, 2, 4, 2), ("z", "x_hi", "x_lo", "y", "core"))
    fsdp, fsdpt = ("z", "x_hi"), ("x_lo", "y", "core")
    both = P(fsdpt, fsdp)
    return jax.shard_map(
        per_device,
        mesh=fine,
        in_specs=(P(fsdpt + fsdp, None), both, both, both, both, both),
        out_specs=(P(fsdpt + fsdp, None), both, both),
        check_vma=False,
    )
```
